256 devices in a mesh: role: 2 (over x_lo), grp: 2 (over x_hi), tp: 64 (over y, z, core).
Axes of the slice: x: 4 (x_hi: 2, x_lo: 2; x = x_hi * 2 + x_lo), y: 4, z: 8, core: 2. Of those that a mesh axis runs over, the one named last changes fastest.
Arguments:
- queries: bfloat16 [2, 8, 8192], P(None, None, ('grp', 'tp')), may hold values from -130 to 130
- step_token_keys: bfloat16 [2, 8, 1024], replicated, may hold values from -6 to 6
- step_token_values: bfloat16 [2, 8, 1024], replicated, may hold values from -6 to 6
- stored_key_cache: bfloat16 [8, 4096, 1024], P(None, ('grp', 'tp')), may hold values from -6 to 6
- stored_value_cache: bfloat16 [8, 4096, 1024], P(None, ('grp', 'tp')), may hold values from -6 to 6
- lengths: int32 [8], replicated, may hold values from 2 to 4096
- wo_sides: bfloat16 [2, 8192, 8192], P('role', ('grp', 'tp')), may hold values from -1 to 1
- gain_sides: float32 [2, 8192], P('role', ('grp', 'tp')), may hold values from 0.5 to 1.5
- head: bfloat16 [8192, 64128], P(None, ('grp', 'tp')), may hold values from -8 to 8
- resid: bfloat16 [2, 8, 8192], P(None, None, ('grp', 'tp')), may hold values from -90 to 90
- actions: int32 [2, 8], replicated, may hold values from 0 to 64127
Outputs:
- log_probs: float32 [2, 8], P('role')
- normed: bfloat16 [2, 8, 8192], P('role', None, ('grp', 'tp'))
The draws below stay inside these ranges and needn't reach their ends.
All inputs are finite; a program needn't handle non-finite values.
Results may differ from the reference program's by a relative error of at most 0.017.
Values may be sent and summed in bfloat16 or wider, within the bound.
No kernel may reach another device: no remote copies, remote signals or barrier semaphores. Data moves between devices by JAX's collectives and lax.ppermute only.
A program may use at most 128 MiB of HBM per device.

```python
import math
import jax
import jax.numpy as jnp
from jax import lax

D = 8192
QUERY_HEADS = 64
KEY_VALUE_HEADS = 8
HEAD_SIZE = 128
V = 64128
DECODED_ROWS = 8
DECODE_STEPS = 2
HD = 8192
CACHE_SLOTS = 4096


def key_table(key):
    return jnp.clip(jax.random.normal(jax.random.fold_in(key, 11), (DECODED_ROWS, CACHE_SLOTS, KEY_VALUE_HEADS * HEAD_SIZE), jnp.float32), -6.0, 6.0)


def draw_stored_key_cache(key, part):
    base_offset = key_table(key)
    return base_offset.astype(jnp.bfloat16)


def draw_queries(key, part):
    drawn = jnp.clip(jax.random.normal(jax.random.fold_in(key, 23), (DECODE_STEPS, DECODED_ROWS, QUERY_HEADS * HEAD_SIZE), jnp.float32), -6.0, 6.0)
    return drawn.astype(jnp.bfloat16)


def draw_resid(key, part):
    noise = jnp.clip(jax.random.normal(jax.random.fold_in(key, 31), (DECODE_STEPS, DECODED_ROWS, D), jnp.float32), -6.0, 6.0)
    ramp = 0.5 + jnp.arange(D, dtype=jnp.float32) / D
    values = noise * ramp[None, None, :]
    return values.astype(jnp.bfloat16)


def draw_head(key, part):
    base_offset = jnp.clip(jax.random.normal(jax.random.fold_in(key, 41), (D, V), jnp.float32), -6.0, 6.0) * (3.0 / math.sqrt(D))
    base_offset = jnp.clip(base_offset, -8.0, 8.0)
    return base_offset.astype(jnp.bfloat16)


def plant(array, stream_key, smallest, high):
    longest = array.shape.index(max(array.shape))
    spots = []
    for shift in (0, 1):
        where = [jax.random.randint(jax.random.fold_in(stream_key, axis), (), 0, length) for axis, length in enumerate(array.shape)]
        where[longest] = (where[longest] + shift) % array.shape[longest]
        spots.append(tuple(where))
    return array.at[spots[0]].set(smallest).at[spots[1]].set(high)


def block_levels(own_key, dims, cuts, smallest, high):
    def one(position, blocks):
        heights = jax.random.uniform(jax.random.fold_in(jax.random.fold_in(own_key, 6), position), (blocks,), jnp.float32, smallest / len(cuts), high / len(cuts))
        return jnp.repeat(jnp.exp(heights), dims[position] // blocks).reshape((-1,) + (1,) * (len(dims) - position - 1))

    level = one(*cuts[0])
    for cut in cuts[1:]:
        level = level * one(*cut)
    return level


def scatter_about(own_key, extent, spread, reach, cuts=(), kind=jnp.bfloat16):
    entries = spread * jax.random.normal(own_key, extent, jnp.float32)
    if cuts:
        entries = entries * block_levels(own_key, extent, cuts, -0.22, 0.18)
    return jnp.clip(entries, -reach, reach).astype(kind)


def setup_inputs(seed: int = 0) -> dict:
    splits = jax.random.split(jax.random.key(seed), 12)
    return {
        "queries": draw_queries(jax.random.fold_in(splits[11], 71), 0),
        "step_token_keys": scatter_about(splits[1], (DECODE_STEPS, DECODED_ROWS, KEY_VALUE_HEADS * HEAD_SIZE), 1.0, 6.0),
        "step_token_values": scatter_about(splits[2], (DECODE_STEPS, DECODED_ROWS, KEY_VALUE_HEADS * HEAD_SIZE), 1.0, 6.0),
        "stored_key_cache": draw_stored_key_cache(jax.random.fold_in(splits[11], 71), 0),
        "stored_value_cache": scatter_about(splits[4], (DECODED_ROWS, CACHE_SLOTS, KEY_VALUE_HEADS * HEAD_SIZE), 1.0, 6.0, ((1, 128),)),
        "lengths": plant(jax.random.randint(splits[5], (DECODED_ROWS,), 2, CACHE_SLOTS + 1), jax.random.fold_in(splits[5], 1), 2, CACHE_SLOTS).astype(jnp.int32),
        "wo_sides": scatter_about(splits[6], (2, HD, D), (max(HD // 256, 1)) ** -0.5, 1.0, ((0, 2), (1, 128))),
        "gain_sides": jnp.clip(1.0 + 0.1 * jax.random.normal(splits[7], (2, D), jnp.float32), 0.5, 1.5),
        "head": draw_head(jax.random.fold_in(splits[11], 71), 0),
        "resid": draw_resid(jax.random.fold_in(splits[11], 71), 0),
        "actions": plant(jax.random.randint(splits[10], (DECODE_STEPS, DECODED_ROWS), 0, V), jax.random.fold_in(splits[10], 1), 0, V - 1).astype(jnp.int32),
    }


def reference(queries, step_token_keys, step_token_values, stored_key_cache, stored_value_cache, lengths, wo_sides, gain_sides, head, resid, actions):
    count_of_rows = lengths.shape[0]
    query_group_width = QUERY_HEADS // KEY_VALUE_HEADS
    logit_scale = 1.0 / math.sqrt(HEAD_SIZE)
    positions = jnp.arange(CACHE_SLOTS, dtype=jnp.int32)
    valid = positions[None, :] < lengths[:, None]
    masking = valid[:, None, None, :]
    prior_keys = stored_key_cache.astype(jnp.float32).reshape(count_of_rows, CACHE_SLOTS, KEY_VALUE_HEADS, HEAD_SIZE)
    prior_values = stored_value_cache.astype(jnp.float32).reshape(count_of_rows, CACHE_SLOTS, KEY_VALUE_HEADS, HEAD_SIZE)
    vocab_ids = jnp.arange(V, dtype=jnp.int32)
    prob_list = []
    normed_list = []
    for decode_index in range(DECODE_STEPS):
        version = 1 - decode_index
        current_query = queries[decode_index].astype(jnp.float32).reshape(count_of_rows, KEY_VALUE_HEADS, query_group_width, HEAD_SIZE) * logit_scale
        scores = jnp.einsum('rkgd,rskd->rkgs', current_query, prior_keys)
        scores = jnp.where(masking, scores, -1e+30)
        incoming_keys = step_token_keys[:decode_index + 1].astype(jnp.float32).reshape(decode_index + 1, count_of_rows, KEY_VALUE_HEADS, HEAD_SIZE)
        incoming_values = step_token_values[:decode_index + 1].astype(jnp.float32).reshape(decode_index + 1, count_of_rows, KEY_VALUE_HEADS, HEAD_SIZE)
        fresh_scores = jnp.einsum('rkgd,trkd->rkgt', current_query, incoming_keys)
        highest = jnp.maximum(lax.optimization_barrier(jnp.max(scores, axis=-1)), lax.optimization_barrier(jnp.max(fresh_scores, axis=-1)))
        cache_probs = jnp.exp(scores - highest[..., None]) * masking
        fresh_probs = jnp.exp(fresh_scores - highest[..., None])
        totals = lax.optimization_barrier(jnp.sum(cache_probs, axis=-1)) + lax.optimization_barrier(jnp.sum(fresh_probs, axis=-1))
        weighted = jnp.einsum('rkgs,rskd->rkgd', cache_probs, prior_values) + jnp.einsum('rkgt,trkd->rkgd', fresh_probs, incoming_values)
        attended = (weighted / totals[..., None]).reshape(count_of_rows, QUERY_HEADS * HEAD_SIZE).astype(jnp.bfloat16)
        state = resid[decode_index].astype(jnp.float32) + jnp.dot(attended, wo_sides[version], preferred_element_type=jnp.float32)
        mean_square = lax.optimization_barrier(jnp.mean(state * state, axis=-1, keepdims=True))
        normed_now = (state * jax.lax.rsqrt(mean_square + 1e-05) * gain_sides[version][None, :]).astype(jnp.bfloat16)
        logits = jnp.dot(normed_now, head, preferred_element_type=jnp.float32)
        largest = lax.optimization_barrier(jnp.max(logits, axis=-1))
        exp_sum = lax.optimization_barrier(jnp.sum(jnp.exp(logits - largest[:, None]), axis=-1))
        is_target = vocab_ids[None, :] == actions[decode_index][:, None]
        target = lax.optimization_barrier(jnp.sum(jnp.where(is_target, logits, 0.0), axis=-1))
        prob_list.append(target - largest - jnp.log(exp_sum))
        normed_list.append(normed_now)
    return (jnp.stack(prob_list), jnp.stack(normed_list))
```

```python
import math

import jax
import jax.numpy as jnp
from jax import lax
from jax.sharding import Mesh
from jax.sharding import PartitionSpec as P

D = 8192
KV_HEADS = 8
GROUP = 8
HEAD_SIZE = 128
CHIP = ("grp", "tp_0", "tp_1")
CORE = "tp_2"
GRP_TP = CHIP + (CORE,)
CHIPS = 64
HALF = 4
LOW = -(2.0**100)
BF = jnp.bfloat16
F32 = jnp.float32


def swap(x):
    return lax.ppermute(x, CORE, [(0, 1), (1, 0)])


def exchange(x, axes):
    return lax.all_to_all(x, axes, split_axis=0, concat_axis=0, tiled=True)


def to_every(x, axes, count):
    return exchange(jnp.broadcast_to(x[None], (count, *x.shape)), axes)


def rounded(x):
    return lax.reduce_precision(x, 8, 7)


def by_core(core, mine, other, axis):
    first = jnp.concatenate([mine, other], axis)
    second = jnp.concatenate([other, mine], axis)
    return jnp.where(core == 0, first, second)


def on_device(
    queries,
    step_token_keys,
    step_token_values,
    stored_key_cache,
    stored_value_cache,
    lengths,
    wo_sides,
    gain_sides,
    head,
    resid,
    actions,
):
    place = lax.axis_index(GRP_TP)
    chip = lax.axis_index(CHIP)
    core = lax.axis_index(CORE)
    side = lax.axis_index("role")
    step = 1 - side
    scale = 1.0 / math.sqrt(HEAD_SIZE)
    slots = stored_key_cache.shape[1]
    row0 = core * HALF
    far0 = (1 - core) * HALF

    def rows_of(x, start, axis=0):
        return lax.dynamic_slice_in_dim(x, start, HALF, axis)

    q_now = lax.dynamic_index_in_dim(queries, step, 0, keepdims=False)
    r_now = lax.dynamic_index_in_dim(resid, step, 0, keepdims=False)
    pair = jnp.stack([q_now, r_now])
    pair_kept = rows_of(pair, row0, 1)
    pair_got = swap(rows_of(pair, far0, 1))
    q_r = by_core(core, pair_kept, pair_got, 2)
    q_chip, r_chip = q_r[0], q_r[1].astype(F32)

    keys = jnp.concatenate(
        [rows_of(stored_key_cache, row0), swap(rows_of(stored_key_cache, far0))], 1
    )
    values = jnp.concatenate(
        [rows_of(stored_value_cache, row0), swap(rows_of(stored_value_cache, far0))], 1
    )
    keys = keys.reshape(HALF, 2 * slots, KV_HEADS, HEAD_SIZE)
    values = values.reshape(HALF, 2 * slots, KV_HEADS, HEAD_SIZE)
    w_mine = wo_sides[0]
    w_far = swap(w_mine)
    gain = gain_sides[0]
    gain_far = swap(gain)
    gain_chip = by_core(core, gain, gain_far, 0)

    q = to_every(q_chip, CHIP, CHIPS)
    q = q.reshape(KV_HEADS, GROUP, HALF, HEAD_SIZE)
    lens = rows_of(lengths, row0)
    at = jnp.arange(slots, dtype=jnp.int32)
    position = jnp.concatenate([place * slots + at, (place + 1 - 2 * core) * slots + at])
    valid = (position[None, :] < lens[:, None])[:, None, None, :]
    scores = jnp.einsum("kgrd,rskd->rkgs", q, keys, preferred_element_type=F32) * scale
    scores = jnp.where(valid, scores, LOW)
    top = rounded(jnp.max(scores, axis=-1, keepdims=True))
    probs = jnp.exp(scores - top) * valid
    total = jnp.sum(probs, axis=-1, keepdims=True)
    part = jnp.einsum(
        "rkgs,rskd->kgrd", probs.astype(BF), values, preferred_element_type=F32
    ).reshape(CHIPS, HALF, HEAD_SIZE)

    def by_head(x):
        return jnp.transpose(x, (1, 2, 0, 3)).reshape(CHIPS, HALF, 1)

    top, total = by_head(top), by_head(total)
    total_hi = rounded(total)
    total_lo = total - total_hi
    gain_hi = rounded(gain_chip)
    gain_pack = jnp.concatenate([gain_hi, gain_chip - gain_hi]).reshape(1, HALF, 64)
    stats = jnp.concatenate(
        [
            jnp.broadcast_to(top, (CHIPS, HALF, 16)),
            jnp.broadcast_to(total_hi, (CHIPS, HALF, 16)),
            jnp.broadcast_to(total_lo, (CHIPS, HALF, 32)),
            jnp.broadcast_to(gain_pack, (CHIPS, HALF, 64)),
        ],
        -1,
    )
    sent = jnp.concatenate([part.astype(BF), stats.astype(BF)], 1)
    got = exchange(sent, CHIP).astype(F32)
    tops, totals = got[:, HALF:, 0:1], got[:, HALF:, 16:17] + got[:, HALF:, 32:33]
    gains = got[:, HALF:, 64:].reshape(CHIPS, 2, HEAD_SIZE).sum(1)
    kv = chip // GROUP
    fresh_k = lax.dynamic_slice(
        step_token_keys, (0, row0, kv * HEAD_SIZE), (2, HALF, HEAD_SIZE)
    ).astype(F32)
    fresh_v = lax.dynamic_slice(
        step_token_values, (0, row0, kv * HEAD_SIZE), (2, HALF, HEAD_SIZE)
    ).astype(F32)
    live = (jnp.arange(2) <= step)[:, None, None]
    fresh_s = jnp.sum(fresh_k * q_chip.astype(F32)[None], -1, keepdims=True) * scale
    fresh_s = jnp.where(live, fresh_s, LOW)
    peak = jnp.maximum(jnp.max(tops, 0), jnp.max(fresh_s, 0))
    factor = jnp.exp(tops - peak[None])
    fresh_p = jnp.exp(fresh_s - peak[None]) * live
    below = jnp.sum(totals * factor, 0) + jnp.sum(fresh_p, 0)
    above = jnp.sum(got[:, :HALF] * factor, 0) + jnp.sum(fresh_p * fresh_v, 0)
    attended = (above / below).astype(BF)

    a0, a1 = attended[:, :64], attended[:, 64:]
    a_mine = jnp.where(core == 0, a0, a1)
    a_far = jnp.where(core == 0, a1, a0)
    share = jnp.dot(a_mine, w_mine, preferred_element_type=F32) + jnp.dot(
        a_far, w_far, preferred_element_type=F32
    )
    share = share.astype(BF).reshape(HALF, CHIPS, HEAD_SIZE).transpose(1, 0, 2)
    state = jnp.sum(exchange(share, CHIP).astype(F32), 0) + r_chip

    mine = to_every(state.astype(BF), CHIP, CHIPS)
    whole = by_core(core, mine, swap(mine), 1).astype(F32)
    square = jnp.sum(jnp.sum(whole * whole, 0), -1, keepdims=True)
    inverse = lax.rsqrt(square / D + 1e-05)
    normed = (whole * inverse[None] * gains[:, None, :]).astype(BF)
    own = lax.dynamic_index_in_dim(normed, chip, 0, keepdims=False)
    own = jnp.where(core == 0, own[:, :64], own[:, 64:])
    to_side = [(0, 1), (1, 0)]
    peer_normed = lax.ppermute(own, "role", to_side)
    logits = jnp.dot(
        normed.transpose(1, 0, 2).reshape(8, D), head, preferred_element_type=F32
    )

    width = head.shape[1]
    action = lax.dynamic_index_in_dim(actions, step, 0, keepdims=False)
    ids = place * width + jnp.arange(width, dtype=jnp.int32)
    target = jnp.sum(jnp.where(ids[None, :] == action[:, None], logits, 0.0), -1)
    high = jnp.max(logits, -1)
    expsum = jnp.sum(jnp.exp(logits - high[:, None]), -1)
    local = jnp.stack([high, expsum, target])
    far = swap(local)
    both = jnp.maximum(local[0], far[0])
    sums = local[1] * jnp.exp(local[0] - both) + far[1] * jnp.exp(far[0] - both)
    packed = jnp.concatenate([both, sums, local[2] + far[2], jnp.zeros_like(sums)])
    heard = to_every(packed[None], ("role",) + CHIP, 2 * CHIPS).reshape(2, CHIPS, 4, 8)
    heard = lax.dynamic_index_in_dim(heard, 1 - side, 0, keepdims=False)
    largest = jnp.max(heard[:, 0], 0)
    sums = jnp.sum(heard[:, 1] * jnp.exp(heard[:, 0] - largest), 0)
    prob = jnp.sum(heard[:, 2], 0) - largest - jnp.log(sums)
    return prob[None], peer_normed[None]


def solution(mesh):
    split = Mesh(
        mesh.devices.reshape(mesh.shape["role"], mesh.shape["grp"], 4, 8, 2),
        ("role", "grp", "tp_0", "tp_1", "tp_2"),
    )
    return jax.shard_map(
        on_device,
        mesh=split,
        in_specs=(
            P(None, None, GRP_TP),
            P(),
            P(),
            P(None, GRP_TP, None),
            P(None, GRP_TP, None),
            P(),
            P("role", GRP_TP, None),
            P("role", GRP_TP),
            P(None, GRP_TP),
            P(None, None, GRP_TP),
            P(),
        ),
        out_specs=(P("role", None), P("role", None, GRP_TP)),
        check_vma=False,
    )
```

```python
import math

import jax
import jax.numpy as jnp
from jax import lax
from jax.experimental import pallas as pl
from jax.experimental.pallas import tpu as pltpu
from jax.sharding import Mesh
from jax.sharding import PartitionSpec as P

D = 8192
KV_HEADS = 8
GROUP = 8
HEAD_SIZE = 128
CHIP = ("grp", "tp_0", "tp_1")
CORE = "tp_2"
GRP_TP = CHIP + (CORE,)
CHIPS = 64
HALF = 4
LOW = -(2.0**100)
BF = jnp.bfloat16
F32 = jnp.float32


def swap(x):
    return lax.ppermute(x, CORE, [(0, 1), (1, 0)])


def exchange(x, axes):
    return lax.all_to_all(x, axes, split_axis=0, concat_axis=0, tiled=True)


def to_every(x, axes, count):
    return exchange(jnp.broadcast_to(x[None], (count, *x.shape)), axes)


def rounded(x):
    return lax.reduce_precision(x, 8, 7)


def by_core(core, mine, other, axis):
    first = jnp.concatenate([mine, other], axis)
    second = jnp.concatenate([other, mine], axis)
    return jnp.where(core == 0, first, second)


NT = (((1,), (1,)), ((), ()))
VMEM = pl.BlockSpec(memory_space=pltpu.VMEM)
SMEM = pl.BlockSpec(memory_space=pltpu.SMEM)


def call(kernel, shapes, specs, limit, cost, *operands):
    return pl.pallas_call(
        kernel,
        out_shape=shapes,
        in_specs=specs,
        out_specs=jax.tree.map(lambda _: VMEM, shapes),
        compiler_params=pltpu.CompilerParams(vmem_limit_bytes=limit * 2**20),
        cost_estimate=pl.CostEstimate(
            flops=cost, bytes_accessed=cost // 16, transcendentals=0
        ),
    )(*operands)


def attend_kernel(core_ref, q_ref, k_ref, kf_ref, v_ref, vf_ref, ok_ref, pack_ref, out_ref):
    base = core_ref[0] * HALF
    row = lax.broadcasted_iota(jnp.int32, (32, 256), 0)
    col = lax.broadcasted_iota(jnp.int32, (32, 256), 1)
    valid = ((row % HALF) == (col // 64)) & (ok_ref[...] > 0)
    lane = lax.broadcasted_iota(jnp.int32, (32, 128), 1)
    upper = lax.broadcasted_iota(jnp.int32, (4, 8, 128), 1) < HALF
    pack = jnp.concatenate([pack_ref[...]] * 4, 0)
    for kv in range(KV_HEADS):
        cols = slice(kv * HEAD_SIZE, (kv + 1) * HEAD_SIZE)

        def both(near, far):
            parts = []
            for r in range(HALF):
                parts += [near[base + r, :, cols], far[base + r, :, cols]]
            return jnp.concatenate(parts, 0)

        q = q_ref[kv * 32 : (kv + 1) * 32, :]
        s = lax.dot_general(q, both(k_ref, kf_ref), NT, preferred_element_type=F32)
        s = jnp.where(valid, s * (1.0 / math.sqrt(HEAD_SIZE)), LOW)
        top = jnp.max(s, 1, keepdims=True).astype(BF).astype(F32)
        p = jnp.where(valid, jnp.exp(s - top), 0.0)
        total = jnp.sum(p, 1, keepdims=True)
        total_hi = total.astype(BF).astype(F32)
        acc = jnp.dot(p.astype(BF), both(v_ref, vf_ref), preferred_element_type=F32)
        stats = jnp.where(lane < 32, total_hi, total - total_hi)
        stats = jnp.where(lane < 16, top, jnp.where(lane < 64, stats, pack))
        acc, stats = acc.reshape(4, 8, 128), stats.reshape(4, 8, 128)
        even = jnp.where(upper, acc, pltpu.roll(stats, HALF, 1)).astype(BF)
        odd = jnp.where(upper, pltpu.roll(acc, HALF, 1), stats).astype(BF)
        for t in range(4):
            out_ref[kv * 8 + 2 * t] = even[t]
            out_ref[kv * 8 + 2 * t + 1] = odd[t]


def merge_kernel(step_ref, got_ref, q_ref, fk_ref, fv_ref, out_ref):
    x = got_ref[...].astype(F32)
    stats = pltpu.roll(x, HALF, 1)
    tops = stats[:, :, 0:1]
    totals = stats[:, :, 16:17] + stats[:, :, 32:33]
    q = q_ref[...]
    scale = 1.0 / math.sqrt(HEAD_SIZE)
    s0 = jnp.sum(fk_ref[0] * q, 1, keepdims=True) * scale
    s1 = jnp.sum(fk_ref[1] * q, 1, keepdims=True) * scale
    second = step_ref[0] >= 1
    s1 = jnp.where(second, s1, LOW)
    peak = jnp.maximum(jnp.max(tops, 0), jnp.maximum(s0, s1))
    factor = jnp.exp(tops - peak[None])
    p0 = jnp.exp(s0 - peak)
    p1 = jnp.where(second, jnp.exp(s1 - peak), 0.0)
    below = jnp.sum(totals * factor, 0) + p0 + p1
    above = jnp.sum(x * factor, 0) + p0 * fv_ref[0] + p1 * fv_ref[1]
    row = lax.broadcasted_iota(jnp.int32, (8, 128), 0)
    out_ref[...] = jnp.where(row < HALF, above / below, 0.0).astype(BF)


def head_kernel(u_ref, head_ref, action_ref, out_ref):
    u = jnp.concatenate([u_ref[i] for i in range(CHIPS)], 1)
    logits = lax.dot_general(head_ref[...], u, NT, preferred_element_type=F32)
    ids = lax.broadcasted_iota(jnp.int32, logits.shape, 0)
    high = jnp.max(logits, 0, keepdims=True)
    out_ref[0:1, :] = high
    out_ref[1:2, :] = jnp.sum(jnp.exp(logits - high), 0, keepdims=True)
    out_ref[2:3, :] = jnp.sum(
        jnp.where(ids == action_ref[...], logits, 0.0), 0, keepdims=True
    )


def on_device(
    queries,
    step_token_keys,
    step_token_values,
    stored_key_cache,
    stored_value_cache,
    lengths,
    wo_sides,
    gain_sides,
    head,
    resid,
    actions,
):
    place = lax.axis_index(GRP_TP)
    chip = lax.axis_index(CHIP)
    core = lax.axis_index(CORE)
    side = lax.axis_index("role")
    step = 1 - side
    slots = stored_key_cache.shape[1]
    row0 = core * HALF

    def rows_of(x, start, axis=0):
        return lax.dynamic_slice_in_dim(x, start, HALF, axis)

    def chip_rows(x, far):
        near = rows_of(lax.dynamic_index_in_dim(x, step, 0, keepdims=False), row0)
        far = rows_of(lax.dynamic_index_in_dim(far, step, 0, keepdims=False), row0)
        return by_core(core, near, far, 1)

    q_chip = chip_rows(queries, swap(queries))
    q = to_every(q_chip, CHIP, CHIPS).reshape(CHIPS * HALF, HEAD_SIZE)

    keys, values, w_mine, gain, resid, lengths, _ = lax.optimization_barrier(
        (stored_key_cache, stored_value_cache, wo_sides[0], gain_sides[0], resid, lengths, q_chip)
    )
    keys_far, values_far, w_far = swap(keys), swap(values), swap(w_mine)
    gain_chip = by_core(core, gain, swap(gain), 0)
    r_chip = chip_rows(resid, swap(resid)).astype(F32)

    lens = rows_of(lengths, row0)
    at = jnp.arange(slots, dtype=jnp.int32)
    position = jnp.concatenate([place * slots + at, (place + 1 - 2 * core) * slots + at])
    valid = (position[None, :] < lens[:, None]).astype(F32).reshape(1, 4 * 2 * slots)
    gain_hi = rounded(gain_chip)
    pack = jnp.concatenate([gain_hi, gain_chip - gain_hi]).reshape(HALF, 64)
    pack = jnp.concatenate([jnp.zeros_like(pack), pack], 1)
    pack = jnp.concatenate([pack, pack], 0)
    sent = call(
        attend_kernel,
        jax.ShapeDtypeStruct((CHIPS, 8, HEAD_SIZE), BF),
        [SMEM] + [VMEM] * 7,
        16,
        2 * 2 * 256 * 256 * 128,
        core[None],
        q,
        keys,
        keys_far,
        values,
        values_far,
        valid,
        pack,
    )
    got = exchange(sent, CHIP)
    gains = got[:, HALF:, 64:].astype(F32).reshape(CHIPS, 2, HEAD_SIZE).sum(1)
    kv = chip // GROUP

    def fresh(x):
        x = lax.dynamic_slice(x, (0, row0, kv * HEAD_SIZE), (2, HALF, HEAD_SIZE))
        return jnp.pad(x.astype(F32), ((0, 0), (0, HALF), (0, 0)))

    attended = call(
        merge_kernel,
        jax.ShapeDtypeStruct((8, HEAD_SIZE), BF),
        [SMEM] + [VMEM] * 4,
        8,
        CHIPS * 8 * HEAD_SIZE * 8,
        step[None],
        got,
        jnp.pad(q_chip.astype(F32), ((0, HALF), (0, 0))),
        fresh(step_token_keys),
        fresh(step_token_values),
    )[:HALF]

    a0, a1 = attended[:, :64], attended[:, 64:]
    a_mine = jnp.where(core == 0, a0, a1)
    a_far = jnp.where(core == 0, a1, a0)
    share = jnp.dot(a_mine, w_mine, preferred_element_type=F32) + jnp.dot(
        a_far, w_far, preferred_element_type=F32
    )
    share = share.astype(BF).reshape(HALF, CHIPS, HEAD_SIZE).transpose(1, 0, 2)
    state = jnp.sum(exchange(share, CHIP).astype(F32), 0) + r_chip

    mine = to_every(state.astype(BF), CHIP, CHIPS)
    whole = by_core(core, mine, swap(mine), 1).astype(F32)
    square = jnp.sum(jnp.sum(whole * whole, 0), -1, keepdims=True)
    inverse = lax.rsqrt(square / D + 1e-05)
    normed = (whole * inverse[None] * gains[:, None, :]).astype(BF)
    own = lax.dynamic_index_in_dim(normed, chip, 0, keepdims=False)
    own = jnp.where(core == 0, own[:, :64], own[:, 64:])
    to_side = [(0, 1), (1, 0)]
    peer_normed = lax.ppermute(own, "role", to_side)
    width = head.shape[1]
    action = lax.dynamic_index_in_dim(actions, step, 0, keepdims=True)
    local = call(
        head_kernel,
        jax.ShapeDtypeStruct((3, 8), F32),
        [VMEM] * 3,
        24,
        2 * 8 * D * width,
        normed,
        head.T,
        action - place * width,
    )
    far = swap(local)
    both = jnp.maximum(local[0], far[0])
    sums = local[1] * jnp.exp(local[0] - both) + far[1] * jnp.exp(far[0] - both)
    packed = jnp.concatenate([both, sums, local[2] + far[2], jnp.zeros_like(sums)])
    heard = to_every(packed[None], ("role",) + CHIP, 2 * CHIPS).reshape(2, CHIPS, 4, 8)
    heard = lax.dynamic_index_in_dim(heard, 1 - side, 0, keepdims=False)
    largest = jnp.max(heard[:, 0], 0)
    sums = jnp.sum(heard[:, 1] * jnp.exp(heard[:, 0] - largest), 0)
    prob = jnp.sum(heard[:, 2], 0) - largest - jnp.log(sums)
    return prob[None], peer_normed[None]


def solution(mesh):
    split = Mesh(
        mesh.devices.reshape(mesh.shape["role"], mesh.shape["grp"], 4, 8, 2),
        ("role", "grp", "tp_0", "tp_1", "tp_2"),
    )
    return jax.shard_map(
        on_device,
        mesh=split,
        in_specs=(
            P(None, None, GRP_TP),
            P(),
            P(),
            P(None, GRP_TP, None),
            P(None, GRP_TP, None),
            P(),
            P("role", GRP_TP, None),
            P("role", GRP_TP),
            P(None, GRP_TP),
            P(None, None, GRP_TP),
            P(),
        ),
        out_specs=(P("role", None), P("role", None, GRP_TP)),
        check_vma=False,
    )
```

```python
import math

import jax
import jax.numpy as jnp
from jax import lax
from jax.experimental import pallas as pl
from jax.experimental.pallas import tpu as pltpu
from jax.sharding import Mesh
from jax.sharding import PartitionSpec as P

D = 8192
KV_HEADS = 8
GROUP = 8
HEAD_SIZE = 128
CHIP = ("grp", "tp_0", "tp_1")
CORE = "tp_2"
GRP_TP = CHIP + (CORE,)
WITHIN = (CORE, "tp_0", "tp_1")
CHIPS = 64
HALF = 4
LOW = -(2.0**100)
BF = jnp.bfloat16
F32 = jnp.float32


def swap(x):
    return lax.ppermute(x, CORE, [(0, 1), (1, 0)])


def exchange(x, axes):
    return lax.all_to_all(x, axes, split_axis=0, concat_axis=0, tiled=True)


def to_every(x, axes, count):
    return exchange(jnp.broadcast_to(x[None], (count, *x.shape)), axes)


def rounded(x):
    return lax.reduce_precision(x, 8, 7)


def by_core(core, mine, other, axis):
    first = jnp.concatenate([mine, other], axis)
    second = jnp.concatenate([other, mine], axis)
    return jnp.where(core == 0, first, second)


NT = (((1,), (1,)), ((), ()))
VMEM = pl.BlockSpec(memory_space=pltpu.VMEM)
SMEM = pl.BlockSpec(memory_space=pltpu.SMEM)


def call(kernel, shapes, specs, limit, cost, *operands):
    return pl.pallas_call(
        kernel,
        out_shape=shapes,
        in_specs=specs,
        out_specs=jax.tree.map(lambda _: VMEM, shapes),
        compiler_params=pltpu.CompilerParams(vmem_limit_bytes=limit * 2**20),
        cost_estimate=pl.CostEstimate(
            flops=cost, bytes_accessed=cost // 16, transcendentals=0
        ),
    )(*operands)


def load_kernel(w_ref, out_ref):
    out_ref[...] = w_ref[...]


def attend_kernel(q_ref, k_ref, v_ref, kf_ref, vf_ref, ok_ref, pack_ref, out_ref):
    x = q_ref[...].astype(F32)
    x0, x1 = x[:128], x[128:]
    left = lax.broadcasted_iota(jnp.int32, (128, 128), 1) < 64
    halves = (
        jnp.where(left, x0, pltpu.roll(x1, 64, 1)).astype(BF),
        jnp.where(left, pltpu.roll(x0, 64, 1), x1).astype(BF),
    )
    row = lax.broadcasted_iota(jnp.int32, (128, 256), 0)
    col = lax.broadcasted_iota(jnp.int32, (128, 256), 1)
    same = (row % HALF) == (col // 64)

    def both(near, far, half, kv):
        cols = slice(kv * HEAD_SIZE, (kv + 1) * HEAD_SIZE)
        parts = []
        for r in range(half * HALF, half * HALF + HALF):
            parts += [near[r, :, cols], far[r, :, cols]]
        return jnp.concatenate(parts, 0)

    scores, valid = [], []
    for half in range(2):
        for kv in range(4):
            q = halves[half][kv * 32 : (kv + 1) * 32]
            scores.append(
                lax.dot_general(q, both(k_ref, kf_ref, half, kv), NT, preferred_element_type=F32)
            )
        valid.append(same & (ok_ref[half : half + 1, :] > 0))
    valid = jnp.concatenate(valid, 0)
    s = jnp.concatenate(scores, 0)
    s = jnp.where(valid, s * (1.0 / math.sqrt(HEAD_SIZE)), LOW)
    top = jnp.max(s, 1, keepdims=True).astype(BF).astype(F32)
    p = jnp.where(valid, jnp.exp(s - top), 0.0)
    total = jnp.sum(p, 1, keepdims=True)
    p = p.astype(BF)
    total_hi = total.astype(BF).astype(F32)
    lane = lax.broadcasted_iota(jnp.int32, (256, 128), 1)
    stats = jnp.where(lane < 32, total_hi, total - total_hi)
    stats = jnp.where(lane < 16, top, stats)
    acc = []
    for half in range(2):
        for kv in range(4):
            n = (half * 4 + kv) * 32
            acc.append(
                jnp.dot(p[n : n + 32], both(v_ref, vf_ref, half, kv), preferred_element_type=F32)
            )
    acc = jnp.concatenate(acc, 0).reshape(32, 8, 128)
    stats = jnp.where(lane.reshape(32, 8, 128) < 64, stats.reshape(32, 8, 128), pack_ref[...][None])
    upper = lax.broadcasted_iota(jnp.int32, (32, 8, 128), 1) < HALF
    even = jnp.where(upper, acc, pltpu.roll(stats, HALF, 1)).astype(BF)
    odd = jnp.where(upper, pltpu.roll(acc, HALF, 1), stats).astype(BF)
    for t in range(32):
        out_ref[2 * t] = even[t]
        out_ref[2 * t + 1] = odd[t]


def merge_kernel(at_ref, got_ref, q_ref, fk_ref, fv_ref, w_ref, far_ref, out_ref):
    x = got_ref[...].astype(F32)
    stats = pltpu.roll(x, HALF, 1)
    tops = stats[:, :, 0:1]
    totals = stats[:, :, 16:17] + stats[:, :, 32:33]
    q = q_ref[...]
    scale = 1.0 / math.sqrt(HEAD_SIZE)
    s0 = jnp.sum(fk_ref[0] * q, 1, keepdims=True) * scale
    s1 = jnp.sum(fk_ref[1] * q, 1, keepdims=True) * scale
    second = at_ref[0] >= 1
    s1 = jnp.where(second, s1, LOW)
    peak = jnp.maximum(jnp.max(tops, 0), jnp.maximum(s0, s1))
    factor = jnp.exp(tops - peak[None])
    p0 = jnp.exp(s0 - peak)
    p1 = jnp.where(second, jnp.exp(s1 - peak), 0.0)
    below = jnp.sum(totals * factor, 0) + p0 + p1
    above = jnp.sum(x * factor, 0) + p0 * fv_ref[0] + p1 * fv_ref[1]
    row = lax.broadcasted_iota(jnp.int32, (8, 128), 0)
    attended = jnp.where(row < HALF, above / below, 0.0)
    turned = pltpu.roll(attended, 64, 1)
    turned = jnp.where(at_ref[1] == 0, attended, turned).astype(BF)
    wide = 1024
    for n in range(0, D, wide):
        w = jnp.concatenate([w_ref[:, n : n + wide], far_ref[:, n : n + wide]], 0)
        share = jnp.dot(turned, w, preferred_element_type=F32)
        for i in range(wide // 128):
            out_ref[n // 128 + i] = share[:HALF, i * 128 : (i + 1) * 128].astype(BF)


def head_kernel(u_ref, head_ref, action_ref, out_ref):
    u = jnp.concatenate([u_ref[i] for i in range(CHIPS)], 1)
    logits = lax.dot_general(head_ref[...], u, NT, preferred_element_type=F32)
    ids = lax.broadcasted_iota(jnp.int32, logits.shape, 0)
    high = jnp.max(logits, 0, keepdims=True)
    out_ref[0:1, :] = high
    out_ref[1:2, :] = jnp.sum(jnp.exp(logits - high), 0, keepdims=True)
    out_ref[2:3, :] = jnp.sum(
        jnp.where(ids == action_ref[...], logits, 0.0), 0, keepdims=True
    )


def on_device(
    queries,
    step_token_keys,
    step_token_values,
    stored_key_cache,
    stored_value_cache,
    lengths,
    wo_sides,
    gain_sides,
    head,
    resid,
    actions,
):
    place = lax.axis_index(GRP_TP)
    chip = lax.axis_index(CHIP)
    core = lax.axis_index(CORE)
    side = lax.axis_index("role")
    step = 1 - side
    slots = stored_key_cache.shape[1]
    row0 = core * HALF

    def rows_of(x, start, axis=0):
        return lax.dynamic_slice_in_dim(x, start, HALF, axis)

    def chip_rows(x, far):
        near = rows_of(lax.dynamic_index_in_dim(x, step, 0, keepdims=False), row0)
        far = rows_of(lax.dynamic_index_in_dim(far, step, 0, keepdims=False), row0)
        return by_core(core, near, far, 1)

    grp = lax.axis_index("grp")
    sides = [(0, 1), (1, 0)]
    away = (1 - grp) * 512
    keys_out = lax.dynamic_slice_in_dim(stored_key_cache, away, 512, 2)
    values_out = lax.dynamic_slice_in_dim(stored_value_cache, away, 512, 2)
    keys_far = lax.ppermute(keys_out, "grp", sides)
    values_far = lax.ppermute(values_out, "grp", sides)
    q_now = lax.dynamic_index_in_dim(queries, step, 0, keepdims=False)
    q_packed = jnp.concatenate([q_now[:HALF], q_now[HALF:]], 1)
    q_packed, _, _ = lax.optimization_barrier((q_packed, keys_out, values_out))
    q = to_every(q_packed, WITHIN, CHIPS).reshape(CHIPS * HALF, HEAD_SIZE)

    keys, values, w_side, gain, resid, queries, lengths, head, _ = lax.optimization_barrier(
        (
            stored_key_cache,
            stored_value_cache,
            wo_sides[0],
            gain_sides,
            resid,
            queries,
            lengths,
            head,
            q_packed,
        )
    )
    keys = lax.dynamic_slice_in_dim(keys, grp * 512, 512, 2)
    values = lax.dynamic_slice_in_dim(values, grp * 512, 512, 2)
    w_mine = call(
        load_kernel,
        jax.ShapeDtypeStruct(w_side.shape, BF),
        [VMEM],
        4,
        1 << 20,
        w_side,
    )
    w_far = swap(w_side)
    head_far = swap(head)
    gain_peer = lax.ppermute(gain, "grp", sides)
    q_chip = chip_rows(queries, swap(queries))
    r_chip = chip_rows(resid, swap(resid)).astype(F32)

    at = jnp.arange(slots, dtype=jnp.int32)
    position = jnp.concatenate([place * slots + at, (place + CHIPS - 2 * CHIPS * grp) * slots + at])
    valid = (position[None, :] < lengths[:, None]).astype(F32).reshape(2, 4 * 2 * slots)
    gain_two = jnp.concatenate([gain, gain_peer], 0)
    gain_hi = rounded(gain_two)
    pack = jnp.concatenate([gain_hi, gain_two - gain_hi], 0)
    pack = jnp.concatenate([jnp.zeros_like(pack), pack], 1)
    pack = jnp.concatenate([pack, pack], 0)
    sent = call(
        attend_kernel,
        jax.ShapeDtypeStruct((CHIPS, 8, HEAD_SIZE), BF),
        [VMEM] * 7,
        16,
        2 * 2 * 256 * 256 * 128,
        q,
        keys,
        values,
        keys_far,
        values_far,
        valid,
        pack,
    )
    got = exchange(sent, WITHIN)
    gains = got[:, HALF:, 64:].astype(F32)
    gains = (gains[:, :2] + gains[:, 2:]).reshape(2, 32, 2, 64)
    gains = gains.transpose(2, 1, 0, 3).reshape(2, 32, HEAD_SIZE)
    gains = jnp.where(grp == 0, gains, gains[::-1]).reshape(CHIPS, HEAD_SIZE)
    kv = chip // GROUP

    def fresh(x):
        x = lax.dynamic_slice(x, (0, row0, kv * HEAD_SIZE), (2, HALF, HEAD_SIZE))
        return jnp.pad(x.astype(F32), ((0, 0), (0, HALF), (0, 0)))

    share = call(
        merge_kernel,
        jax.ShapeDtypeStruct((CHIPS, HALF, HEAD_SIZE), BF),
        [SMEM] + [VMEM] * 6,
        16,
        2 * 8 * HEAD_SIZE * D,
        jnp.stack([step, core]),
        got,
        jnp.pad(q_chip.astype(F32), ((0, HALF), (0, 0))),
        fresh(step_token_keys),
        fresh(step_token_values),
        w_mine,
        w_far,
    )
    state = jnp.sum(exchange(share, CHIP).astype(F32), 0) + r_chip

    mine = to_every(state.astype(BF), CHIP, CHIPS)
    whole = by_core(core, mine, swap(mine), 1).astype(F32)
    square = jnp.sum(jnp.sum(whole * whole, 0), -1, keepdims=True)
    inverse = lax.rsqrt(square / D + 1e-05)
    normed = (whole * inverse[None] * gains[:, None, :]).astype(BF)
    own = lax.dynamic_index_in_dim(normed, chip, 0, keepdims=False)
    own = jnp.where(core == 0, own[:, :64], own[:, 64:])
    to_side = [(0, 1), (1, 0)]
    peer_normed = lax.ppermute(own, "role", to_side)
    width = head.shape[1]
    action = lax.dynamic_index_in_dim(actions, step, 0, keepdims=True)
    local = call(
        head_kernel,
        jax.ShapeDtypeStruct((3, 8), F32),
        [VMEM] * 3,
        24,
        2 * 8 * D * width,
        normed,
        head_far.T,
        action - (place + 1 - 2 * core) * width,
    )
    far = swap(local)
    both = jnp.maximum(local[0], far[0])
    sums = local[1] * jnp.exp(local[0] - both) + far[1] * jnp.exp(far[0] - both)
    packed = jnp.concatenate([both, sums, local[2] + far[2], jnp.zeros_like(sums)])
    heard = to_every(packed[None], ("role",) + CHIP, 2 * CHIPS).reshape(2, CHIPS, 4, 8)
    heard = lax.dynamic_index_in_dim(heard, 1 - side, 0, keepdims=False)
    largest = jnp.max(heard[:, 0], 0)
    sums = jnp.sum(heard[:, 1] * jnp.exp(heard[:, 0] - largest), 0)
    prob = jnp.sum(heard[:, 2], 0) - largest - jnp.log(sums)
    return prob[None], peer_normed[None]


def solution(mesh):
    split = Mesh(
        mesh.devices.reshape(mesh.shape["role"], mesh.shape["grp"], 4, 8, 2),
        ("role", "grp", "tp_0", "tp_1", "tp_2"),
    )
    return jax.shard_map(
        on_device,
        mesh=split,
        in_specs=(
            P(None, None, GRP_TP),
            P(),
            P(),
            P(None, GRP_TP, None),
            P(None, GRP_TP, None),
            P(),
            P("role", GRP_TP, None),
            P("role", GRP_TP),
            P(None, GRP_TP),
            P(None, None, GRP_TP),
            P(),
        ),
        out_specs=(P("role", None), P("role", None, GRP_TP)),
        check_vma=False,
    )
```

```python
import math

import jax
import jax.numpy as jnp
from jax import lax
from jax.experimental import pallas as pl
from jax.experimental.pallas import tpu as pltpu
from jax.sharding import Mesh
from jax.sharding import PartitionSpec as P

D = 8192
KV_HEADS = 8
GROUP = 8
HEAD_SIZE = 128
CHIP = ("grp", "tp_0", "tp_1")
CORE = "tp_2"
GRP_TP = CHIP + (CORE,)
CHIPS = 64
HALF = 4
LOW = -(2.0**100)
BF = jnp.bfloat16
F32 = jnp.float32


def swap(x):
    return lax.ppermute(x, CORE, [(0, 1), (1, 0)])


def exchange(x, axes):
    return lax.all_to_all(x, axes, split_axis=0, concat_axis=0, tiled=True)


def to_every(x, axes, count):
    return exchange(jnp.broadcast_to(x[None], (count, *x.shape)), axes)


def rounded(x):
    return lax.reduce_precision(x, 8, 7)


def by_core(core, mine, other, axis):
    first = jnp.concatenate([mine, other], axis)
    second = jnp.concatenate([other, mine], axis)
    return jnp.where(core == 0, first, second)


NT = (((1,), (1,)), ((), ()))
VMEM = pl.BlockSpec(memory_space=pltpu.VMEM)
SMEM = pl.BlockSpec(memory_space=pltpu.SMEM)


def call(kernel, shapes, specs, limit, cost, *operands):
    return pl.pallas_call(
        kernel,
        out_shape=shapes,
        in_specs=specs,
        out_specs=jax.tree.map(lambda _: VMEM, shapes),
        compiler_params=pltpu.CompilerParams(vmem_limit_bytes=limit * 2**20),
        cost_estimate=pl.CostEstimate(
            flops=cost, bytes_accessed=cost // 16, transcendentals=0
        ),
    )(*operands)


def first_kernel(at_ref, near_ref, far_ref, out_ref, chip_ref):
    step, first = at_ref[0], at_ref[1] == 0
    near = near_ref[step].astype(F32)
    far = far_ref[step].astype(F32)
    x = jnp.concatenate([near, far], 1)
    x = jnp.where(first, x, pltpu.roll(x, 64, 1))
    x = jnp.where(first, x, pltpu.roll(x, HALF, 0))
    row = lax.broadcasted_iota(jnp.int32, (8, 128), 0)
    chip_ref[...] = jnp.where(row < HALF, x, 0.0)
    out_ref[...] = jnp.broadcast_to(x[:HALF].astype(BF)[None], out_ref.shape)


def load_kernel(x_ref, out_ref):
    out_ref[...] = x_ref[...]


def attend_kernel(core_ref, q_ref, k_ref, v_ref, kf_ref, vf_ref, ok_ref, pack_ref, out_ref):
    base = core_ref[0] * HALF
    row = lax.broadcasted_iota(jnp.int32, (256, 256), 0)
    col = lax.broadcasted_iota(jnp.int32, (256, 256), 1)
    valid = ((row % HALF) == (col // 64)) & (ok_ref[...] > 0)

    def both(near, far, kv):
        cols = slice(kv * HEAD_SIZE, (kv + 1) * HEAD_SIZE)
        parts = []
        for r in range(HALF):
            parts += [near[r, :, cols], far[base + r, :, cols]]
        return jnp.concatenate(parts, 0)

    s = jnp.concatenate(
        [
            lax.dot_general(
                q_ref[kv * 32 : (kv + 1) * 32, :],
                both(k_ref, kf_ref, kv),
                NT,
                preferred_element_type=F32,
            )
            for kv in range(KV_HEADS)
        ],
        0,
    )
    s = jnp.where(valid, s * (1.0 / math.sqrt(HEAD_SIZE)), LOW)
    top = jnp.max(s, 1, keepdims=True).astype(BF).astype(F32)
    p = jnp.where(valid, jnp.exp(s - top), 0.0)
    total = jnp.sum(p, 1, keepdims=True)
    p = p.astype(BF)
    total_hi = total.astype(BF).astype(F32)
    lane = lax.broadcasted_iota(jnp.int32, (256, 128), 1)
    stats = jnp.where(lane < 32, total_hi, total - total_hi)
    stats = jnp.where(lane < 16, top, stats)
    acc = jnp.concatenate(
        [
            jnp.dot(
                p[kv * 32 : (kv + 1) * 32],
                both(v_ref, vf_ref, kv),
                preferred_element_type=F32,
            )
            for kv in range(KV_HEADS)
        ],
        0,
    ).reshape(32, 8, 128)
    stats = jnp.where(lane.reshape(32, 8, 128) < 64, stats.reshape(32, 8, 128), pack_ref[...][None])
    upper = lax.broadcasted_iota(jnp.int32, (32, 8, 128), 1) < HALF
    even = jnp.where(upper, acc, pltpu.roll(stats, HALF, 1)).astype(BF)
    odd = jnp.where(upper, pltpu.roll(acc, HALF, 1), stats).astype(BF)
    for t in range(32):
        out_ref[2 * t] = even[t]
        out_ref[2 * t + 1] = odd[t]


def merge_kernel(at_ref, got_ref, q_ref, fk_ref, fv_ref, w_ref, far_ref, out_ref):
    x = got_ref[...].astype(F32)
    stats = pltpu.roll(x, HALF, 1)
    tops = stats[:, :, 0:1]
    totals = stats[:, :, 16:17] + stats[:, :, 32:33]
    q = q_ref[...]
    scale = 1.0 / math.sqrt(HEAD_SIZE)
    s0 = jnp.sum(fk_ref[0] * q, 1, keepdims=True) * scale
    s1 = jnp.sum(fk_ref[1] * q, 1, keepdims=True) * scale
    second = at_ref[0] >= 1
    s1 = jnp.where(second, s1, LOW)
    peak = jnp.maximum(jnp.max(tops, 0), jnp.maximum(s0, s1))
    factor = jnp.exp(tops - peak[None])
    p0 = jnp.exp(s0 - peak)
    p1 = jnp.where(second, jnp.exp(s1 - peak), 0.0)
    below = jnp.sum(totals * factor, 0) + p0 + p1
    above = jnp.sum(x * factor, 0) + p0 * fv_ref[0] + p1 * fv_ref[1]
    row = lax.broadcasted_iota(jnp.int32, (8, 128), 0)
    attended = jnp.where(row < HALF, above / below, 0.0)
    turned = pltpu.roll(attended, 64, 1)
    turned = jnp.where(at_ref[1] == 0, attended, turned).astype(BF)
    wide = 1024
    for n in range(0, D, wide):
        w = jnp.concatenate([w_ref[:, n : n + wide], far_ref[:, n : n + wide]], 0)
        share = jnp.dot(turned, w, preferred_element_type=F32)
        for i in range(wide // 128):
            out_ref[n // 128 + i] = share[:HALF, i * 128 : (i + 1) * 128].astype(BF)


def state_kernel(got_ref, resid_ref, out_ref):
    state = jnp.sum(got_ref[...].astype(F32), 0) + resid_ref[...]
    out_ref[...] = jnp.broadcast_to(state.astype(BF)[None], out_ref.shape)


def head_kernel(u_ref, head_ref, action_ref, out_ref):
    u = jnp.concatenate([u_ref[i] for i in range(CHIPS)], 1)
    logits = lax.dot_general(head_ref[...], u, NT, preferred_element_type=F32)
    ids = lax.broadcasted_iota(jnp.int32, logits.shape, 0)
    high = jnp.max(logits, 0, keepdims=True)
    out_ref[...] = jnp.zeros_like(out_ref)
    out_ref[0:1, 0:8] = high
    out_ref[1:2, 0:8] = jnp.sum(jnp.exp(logits - high), 0, keepdims=True)
    out_ref[2:3, 0:8] = jnp.sum(
        jnp.where(ids == action_ref[...], logits, 0.0), 0, keepdims=True
    )


def pack_kernel(near_ref, far_ref, out_ref):
    a, b = near_ref[...], far_ref[...]
    high = jnp.maximum(a[0:1], b[0:1])
    total = a[1:2] * jnp.exp(a[0:1] - high) + b[1:2] * jnp.exp(b[0:1] - high)
    x = high + pltpu.roll(total, 8, 1) + pltpu.roll(a[2:3] + b[2:3], 16, 1)
    out_ref[...] = jnp.broadcast_to(x[None], out_ref.shape)


def final_kernel(start_ref, heard_ref, out_ref):
    x = heard_ref[pl.ds(start_ref[0], CHIPS)]
    high = jnp.max(x, 0, keepdims=True)
    total = jnp.sum(pltpu.roll(x, 120, 2) * jnp.exp(x - high), 0)
    target = jnp.sum(pltpu.roll(x, 112, 2), 0)
    out_ref[...] = (target - high[0] - jnp.log(total))[:, 0:8]


def on_device(
    queries,
    step_token_keys,
    step_token_values,
    stored_key_cache,
    stored_value_cache,
    lengths,
    wo_sides,
    gain_sides,
    head,
    resid,
    actions,
):
    place = lax.axis_index(GRP_TP)
    chip = lax.axis_index(CHIP)
    core = lax.axis_index(CORE)
    side = lax.axis_index("role")
    step = 1 - side
    slots = stored_key_cache.shape[1]
    row0 = core * HALF

    def rows_of(x, start, axis=0):
        return lax.dynamic_slice_in_dim(x, start, HALF, axis)

    def chip_rows(x, far):
        near = rows_of(lax.dynamic_index_in_dim(x, step, 0, keepdims=False), row0)
        far = rows_of(lax.dynamic_index_in_dim(far, step, 0, keepdims=False), row0)
        return by_core(core, near, far, 1)

    spot = jnp.stack([step, core])
    sent, q_chip = call(
        first_kernel,
        (
            jax.ShapeDtypeStruct((CHIPS, HALF, HEAD_SIZE), BF),
            jax.ShapeDtypeStruct((8, HEAD_SIZE), F32),
        ),
        [SMEM, VMEM, VMEM],
        4,
        1 << 16,
        spot,
        queries,
        swap(queries),
    )
    q = exchange(sent, CHIP).reshape(CHIPS * HALF, HEAD_SIZE)

    keys, values, gain, lengths, _ = lax.optimization_barrier(
        (stored_key_cache, stored_value_cache, gain_sides[0], lengths, q_chip)
    )
    keys_far, values_far = swap(keys), swap(values)
    keys, values = rows_of(keys, row0), rows_of(values, row0)
    gain_chip = by_core(core, gain, swap(gain), 0)

    lens = rows_of(lengths, row0)
    at = jnp.arange(slots, dtype=jnp.int32)
    position = jnp.concatenate([place * slots + at, (place + 1 - 2 * core) * slots + at])
    valid = (position[None, :] < lens[:, None]).astype(F32).reshape(1, 4 * 2 * slots)
    gain_hi = rounded(gain_chip)
    pack = jnp.concatenate([gain_hi, gain_chip - gain_hi]).reshape(HALF, 64)
    pack = jnp.concatenate([jnp.zeros_like(pack), pack], 1)
    pack = jnp.concatenate([pack, pack], 0)
    sent = call(
        attend_kernel,
        jax.ShapeDtypeStruct((CHIPS, 8, HEAD_SIZE), BF),
        [SMEM] + [VMEM] * 7,
        16,
        2 * 2 * 256 * 256 * 128,
        core[None],
        q,
        keys,
        values,
        keys_far,
        values_far,
        valid,
        pack,
    )
    got = exchange(sent, CHIP)
    w_side, resid, new_keys, new_values, _ = lax.optimization_barrier(
        (wo_sides[0], resid, step_token_keys, step_token_values, sent)
    )
    w_far = swap(w_side)
    w_mine = call(load_kernel, jax.ShapeDtypeStruct(w_side.shape, BF), [VMEM], 8, 1 << 20, w_side)
    r_chip = chip_rows(resid, swap(resid)).astype(F32)
    gains = got[:, HALF:, 64:].astype(F32).reshape(CHIPS, 2, HEAD_SIZE).sum(1)
    kv = chip // GROUP

    def fresh(x):
        x = lax.dynamic_slice(x, (0, row0, kv * HEAD_SIZE), (2, HALF, HEAD_SIZE))
        return jnp.pad(x.astype(F32), ((0, 0), (0, HALF), (0, 0)))

    share = call(
        merge_kernel,
        jax.ShapeDtypeStruct((CHIPS, HALF, HEAD_SIZE), BF),
        [SMEM] + [VMEM] * 6,
        16,
        2 * 8 * HEAD_SIZE * D,
        spot,
        got,
        q_chip,
        fresh(new_keys),
        fresh(new_values),
        w_mine,
        w_far,
    )
    shares = exchange(share, CHIP)
    head_t, actions, _ = lax.optimization_barrier((head.T, actions, share))
    head_t = call(load_kernel, jax.ShapeDtypeStruct(head_t.shape, BF), [VMEM], 24, 1 << 24, head_t)
    sent = call(
        state_kernel,
        jax.ShapeDtypeStruct((CHIPS, HALF, HEAD_SIZE), BF),
        [VMEM, VMEM],
        4,
        1 << 16,
        shares,
        r_chip,
    )
    mine = exchange(sent, CHIP)
    whole = by_core(core, mine, swap(mine), 1).astype(F32)
    square = jnp.sum(jnp.sum(whole * whole, 0), -1, keepdims=True)
    inverse = lax.rsqrt(square / D + 1e-05)
    normed = (whole * inverse[None] * gains[:, None, :]).astype(BF)
    own = lax.dynamic_index_in_dim(normed, chip, 0, keepdims=False)
    own = jnp.where(core == 0, own[:, :64], own[:, 64:])
    to_side = [(0, 1), (1, 0)]
    peer_normed = lax.ppermute(own, "role", to_side)
    width = head.shape[1]
    action = lax.dynamic_index_in_dim(actions, step, 0, keepdims=True)
    local = call(
        head_kernel,
        jax.ShapeDtypeStruct((8, 128), F32),
        [VMEM] * 3,
        24,
        2 * 8 * D * width,
        normed,
        head_t,
        action - place * width,
    )
    packed = call(
        pack_kernel,
        jax.ShapeDtypeStruct((2 * CHIPS, 1, HEAD_SIZE), F32),
        [VMEM, VMEM],
        4,
        1 << 16,
        local,
        swap(local),
    )
    heard = exchange(packed, ("role",) + CHIP)
    prob = call(
        final_kernel,
        jax.ShapeDtypeStruct((1, 8), F32),
        [SMEM, VMEM],
        4,
        1 << 16,
        ((1 - side) * CHIPS)[None],
        heard,
    )
    return prob, peer_normed[None]


def solution(mesh):
    split = Mesh(
        mesh.devices.reshape(mesh.shape["role"], mesh.shape["grp"], 4, 8, 2),
        ("role", "grp", "tp_0", "tp_1", "tp_2"),
    )
    return jax.shard_map(
        on_device,
        mesh=split,
        in_specs=(
            P(None, None, GRP_TP),
            P(),
            P(),
            P(None, GRP_TP, None),
            P(None, GRP_TP, None),
            P(),
            P("role", GRP_TP, None),
            P("role", GRP_TP),
            P(None, GRP_TP),
            P(None, None, GRP_TP),
            P(),
        ),
        out_specs=(P("role", None), P("role", None, GRP_TP)),
        check_vma=False,
    )
```

```python
import math

import jax
import jax.numpy as jnp
from jax import lax
from jax.experimental import pallas as pl
from jax.experimental.pallas import tpu as pltpu
from jax.sharding import Mesh
from jax.sharding import PartitionSpec as P

D = 8192
KV_HEADS = 8
GROUP = 8
HEAD_SIZE = 128
CHIP = ("grp", "tp_0", "tp_1")
CORE = "tp_2"
GRP_TP = CHIP + (CORE,)
CHIPS = 64
HALF = 4
LOW = -(2.0**100)
BF = jnp.bfloat16
F32 = jnp.float32


def swap(x):
    return lax.ppermute(x, CORE, [(0, 1), (1, 0)])


def exchange(x, axes):
    return lax.all_to_all(x, axes, split_axis=0, concat_axis=0, tiled=True)


def rounded(x):
    return lax.reduce_precision(x, 8, 7)


def by_core(core, mine, other, axis):
    first = jnp.concatenate([mine, other], axis)
    second = jnp.concatenate([other, mine], axis)
    return jnp.where(core == 0, first, second)


NT = (((1,), (1,)), ((), ()))
VMEM = pl.BlockSpec(memory_space=pltpu.VMEM)
SMEM = pl.BlockSpec(memory_space=pltpu.SMEM)


def call(kernel, shapes, specs, limit, cost, *operands):
    return pl.pallas_call(
        kernel,
        out_shape=shapes,
        in_specs=specs,
        out_specs=jax.tree.map(lambda _: VMEM, shapes),
        compiler_params=pltpu.CompilerParams(vmem_limit_bytes=limit * 2**20),
        cost_estimate=pl.CostEstimate(
            flops=cost, bytes_accessed=cost // 16, transcendentals=0
        ),
    )(*operands)


def load_kernel(x_ref, out_ref):
    out_ref[...] = x_ref[...]


def attend_kernel(core_ref, q_ref, k_ref, v_ref, kf_ref, vf_ref, ok_ref, pack_ref, out_ref):
    base = core_ref[0] * HALF
    row = lax.broadcasted_iota(jnp.int32, (256, 256), 0)
    col = lax.broadcasted_iota(jnp.int32, (256, 256), 1)
    valid = ((row % HALF) == (col // 64)) & (ok_ref[...] > 0)

    def both(near, far, kv):
        cols = slice(kv * HEAD_SIZE, (kv + 1) * HEAD_SIZE)
        parts = []
        for r in range(HALF):
            parts += [near[r, :, cols], far[base + r, :, cols]]
        return jnp.concatenate(parts, 0)

    s = jnp.concatenate(
        [
            lax.dot_general(
                q_ref[kv * 32 : (kv + 1) * 32, :],
                both(k_ref, kf_ref, kv),
                NT,
                preferred_element_type=F32,
            )
            for kv in range(KV_HEADS)
        ],
        0,
    )
    s = jnp.where(valid, s * (1.0 / math.sqrt(HEAD_SIZE)), LOW)
    top = jnp.max(s, 1, keepdims=True).astype(BF).astype(F32)
    p = jnp.where(valid, jnp.exp(s - top), 0.0)
    total = jnp.sum(p, 1, keepdims=True)
    p = p.astype(BF)
    total_hi = total.astype(BF).astype(F32)
    lane = lax.broadcasted_iota(jnp.int32, (256, 128), 1)
    stats = jnp.where(lane < 32, total_hi, total - total_hi)
    stats = jnp.where(lane < 16, top, stats)
    acc = jnp.concatenate(
        [
            jnp.dot(
                p[kv * 32 : (kv + 1) * 32],
                both(v_ref, vf_ref, kv),
                preferred_element_type=F32,
            )
            for kv in range(KV_HEADS)
        ],
        0,
    ).reshape(32, 8, 128)
    stats = jnp.where(lane.reshape(32, 8, 128) < 64, stats.reshape(32, 8, 128), pack_ref[...][None])
    upper = lax.broadcasted_iota(jnp.int32, (32, 8, 128), 1) < HALF
    even = jnp.where(upper, acc, pltpu.roll(stats, HALF, 1)).astype(BF)
    odd = jnp.where(upper, pltpu.roll(acc, HALF, 1), stats).astype(BF)
    for t in range(32):
        out_ref[2 * t] = even[t]
        out_ref[2 * t + 1] = odd[t]


def merge_kernel(at_ref, got_ref, q_ref, fk_ref, fv_ref, w_ref, far_ref, out_ref):
    x = got_ref[...].astype(F32)
    stats = pltpu.roll(x, HALF, 1)
    tops = stats[:, :, 0:1]
    totals = stats[:, :, 16:17] + stats[:, :, 32:33]
    q = q_ref[...]
    scale = 1.0 / math.sqrt(HEAD_SIZE)
    s0 = jnp.sum(fk_ref[0] * q, 1, keepdims=True) * scale
    s1 = jnp.sum(fk_ref[1] * q, 1, keepdims=True) * scale
    second = at_ref[0] >= 1
    s1 = jnp.where(second, s1, LOW)
    peak = jnp.maximum(jnp.max(tops, 0), jnp.maximum(s0, s1))
    factor = jnp.exp(tops - peak[None])
    p0 = jnp.exp(s0 - peak)
    p1 = jnp.where(second, jnp.exp(s1 - peak), 0.0)
    below = jnp.sum(totals * factor, 0) + p0 + p1
    above = jnp.sum(x * factor, 0) + p0 * fv_ref[0] + p1 * fv_ref[1]
    row = lax.broadcasted_iota(jnp.int32, (8, 128), 0)
    attended = jnp.where(row < HALF, above / below, 0.0)
    turned = pltpu.roll(attended, 64, 1)
    turned = jnp.where(at_ref[1] == 0, attended, turned).astype(BF)
    wide = 1024
    for n in range(0, D, wide):
        w = jnp.concatenate([w_ref[:, n : n + wide], far_ref[:, n : n + wide]], 0)
        share = jnp.dot(turned, w, preferred_element_type=F32)
        for i in range(wide // 128):
            out_ref[n // 128 + i] = share[:HALF, i * 128 : (i + 1) * 128].astype(BF)


def state_kernel(got_ref, resid_ref, out_ref):
    state = jnp.sum(got_ref[...].astype(F32), 0) + resid_ref[...]
    out_ref[...] = jnp.broadcast_to(state.astype(BF)[None], out_ref.shape)


def head_kernel(u_ref, head_ref, action_ref, out_ref):
    u = jnp.concatenate([u_ref[i] for i in range(CHIPS)], 1)
    logits = lax.dot_general(head_ref[...], u, NT, preferred_element_type=F32)
    ids = lax.broadcasted_iota(jnp.int32, logits.shape, 0)
    high = jnp.max(logits, 0, keepdims=True)
    out_ref[...] = jnp.zeros_like(out_ref)
    out_ref[0:1, 0:8] = high
    out_ref[1:2, 0:8] = jnp.sum(jnp.exp(logits - high), 0, keepdims=True)
    out_ref[2:3, 0:8] = jnp.sum(
        jnp.where(ids == action_ref[...], logits, 0.0), 0, keepdims=True
    )


def pack_kernel(near_ref, far_ref, out_ref):
    a, b = near_ref[...], far_ref[...]
    high = jnp.maximum(a[0:1], b[0:1])
    total = a[1:2] * jnp.exp(a[0:1] - high) + b[1:2] * jnp.exp(b[0:1] - high)
    x = high + pltpu.roll(total, 8, 1) + pltpu.roll(a[2:3] + b[2:3], 16, 1)
    out_ref[...] = jnp.broadcast_to(x[None], out_ref.shape)


def final_kernel(start_ref, heard_ref, out_ref):
    x = heard_ref[pl.ds(start_ref[0], CHIPS)]
    high = jnp.max(x, 0, keepdims=True)
    total = jnp.sum(pltpu.roll(x, 120, 2) * jnp.exp(x - high), 0)
    target = jnp.sum(pltpu.roll(x, 112, 2), 0)
    out_ref[...] = (target - high[0] - jnp.log(total))[:, 0:8]


def on_device(
    queries,
    step_token_keys,
    step_token_values,
    stored_key_cache,
    stored_value_cache,
    lengths,
    wo_sides,
    gain_sides,
    head,
    resid,
    actions,
):
    place = lax.axis_index(GRP_TP)
    chip = lax.axis_index(CHIP)
    core = lax.axis_index(CORE)
    side = lax.axis_index("role")
    step = 1 - side
    slots = stored_key_cache.shape[1]
    row0 = core * HALF

    def rows_of(x, start, axis=0):
        return lax.dynamic_slice_in_dim(x, start, HALF, axis)

    def chip_rows(x, far):
        near = rows_of(lax.dynamic_index_in_dim(x, step, 0, keepdims=False), row0)
        far = rows_of(lax.dynamic_index_in_dim(far, step, 0, keepdims=False), row0)
        return by_core(core, near, far, 1)

    spot = jnp.stack([step, core])
    q_half = chip_rows(queries, swap(queries))
    q_chip = jnp.pad(q_half.astype(F32), ((0, HALF), (0, 0)))
    q = exchange(jnp.broadcast_to(q_half[None], (CHIPS, *q_half.shape)), CHIP)
    q = q.reshape(CHIPS * HALF, HEAD_SIZE)

    keys, values, gain, lengths, _ = lax.optimization_barrier(
        (stored_key_cache, stored_value_cache, gain_sides[0], lengths, q_half)
    )
    keys_far, values_far = swap(keys), swap(values)
    keys, values = rows_of(keys, row0), rows_of(values, row0)
    gain_chip = by_core(core, gain, swap(gain), 0)

    lens = rows_of(lengths, row0)
    at = jnp.arange(slots, dtype=jnp.int32)
    position = jnp.concatenate([place * slots + at, (place + 1 - 2 * core) * slots + at])
    valid = (position[None, :] < lens[:, None]).astype(F32).reshape(1, 4 * 2 * slots)
    gain_hi = rounded(gain_chip)
    pack = jnp.concatenate([gain_hi, gain_chip - gain_hi]).reshape(HALF, 64)
    pack = jnp.concatenate([jnp.zeros_like(pack), pack], 1)
    pack = jnp.concatenate([pack, pack], 0)
    sent = call(
        attend_kernel,
        jax.ShapeDtypeStruct((CHIPS, 8, HEAD_SIZE), BF),
        [SMEM] + [VMEM] * 7,
        16,
        2 * 2 * 256 * 256 * 128,
        core[None],
        q,
        keys,
        values,
        keys_far,
        values_far,
        valid,
        pack,
    )
    got = exchange(sent, CHIP)
    w_side, resid, new_keys, new_values, _ = lax.optimization_barrier(
        (wo_sides[0], resid, step_token_keys, step_token_values, sent)
    )
    w_far = swap(w_side)
    w_mine = call(load_kernel, jax.ShapeDtypeStruct(w_side.shape, BF), [VMEM], 8, 1 << 20, w_side)
    r_chip = chip_rows(resid, swap(resid)).astype(F32)
    gains = got[:, HALF:, 64:].astype(F32).reshape(CHIPS, 2, HEAD_SIZE).sum(1)
    kv = chip // GROUP

    def fresh(x):
        x = lax.dynamic_slice(x, (0, row0, kv * HEAD_SIZE), (2, HALF, HEAD_SIZE))
        return jnp.pad(x.astype(F32), ((0, 0), (0, HALF), (0, 0)))

    share = call(
        merge_kernel,
        jax.ShapeDtypeStruct((CHIPS, HALF, HEAD_SIZE), BF),
        [SMEM] + [VMEM] * 6,
        16,
        2 * 8 * HEAD_SIZE * D,
        jnp.stack([step, core]),
        got,
        q_chip,
        fresh(new_keys),
        fresh(new_values),
        w_mine,
        w_far,
    )
    shares = exchange(share, CHIP)
    sent = call(
        state_kernel,
        jax.ShapeDtypeStruct((CHIPS, HALF, HEAD_SIZE), BF),
        [VMEM, VMEM],
        4,
        1 << 16,
        shares,
        r_chip,
    )
    mine = exchange(sent, CHIP)
    whole = by_core(core, mine, swap(mine), 1).astype(F32)
    square = jnp.sum(jnp.sum(whole * whole, 0), -1, keepdims=True)
    inverse = lax.rsqrt(square / D + 1e-05)
    normed = (whole * inverse[None] * gains[:, None, :]).astype(BF)
    own = lax.dynamic_index_in_dim(normed, chip, 0, keepdims=False)
    own = jnp.where(core == 0, own[:, :64], own[:, 64:])
    to_side = [(0, 1), (1, 0)]
    peer_normed = lax.ppermute(own, "role", to_side)
    width = head.shape[1]
    action = lax.dynamic_index_in_dim(actions, step, 0, keepdims=True)
    local = call(
        head_kernel,
        jax.ShapeDtypeStruct((8, 128), F32),
        [VMEM] * 3,
        24,
        2 * 8 * D * width,
        normed,
        head.T,
        action - place * width,
    )
    packed = call(
        pack_kernel,
        jax.ShapeDtypeStruct((2 * CHIPS, 1, HEAD_SIZE), F32),
        [VMEM, VMEM],
        4,
        1 << 16,
        local,
        swap(local),
    )
    heard = exchange(packed, ("role",) + CHIP)
    prob = call(
        final_kernel,
        jax.ShapeDtypeStruct((1, 8), F32),
        [SMEM, VMEM],
        4,
        1 << 16,
        ((1 - side) * CHIPS)[None],
        heard,
    )
    return prob, peer_normed[None]


def solution(mesh):
    split = Mesh(
        mesh.devices.reshape(mesh.shape["role"], mesh.shape["grp"], 4, 8, 2),
        ("role", "grp", "tp_0", "tp_1", "tp_2"),
    )
    return jax.shard_map(
        on_device,
        mesh=split,
        in_specs=(
            P(None, None, GRP_TP),
            P(),
            P(),
            P(None, GRP_TP, None),
            P(None, GRP_TP, None),
            P(),
            P("role", GRP_TP, None),
            P("role", GRP_TP),
            P(None, GRP_TP),
            P(None, None, GRP_TP),
            P(),
        ),
        out_specs=(P("role", None), P("role", None, GRP_TP)),
        check_vma=False,
    )
```

```python
import math

import jax
import jax.numpy as jnp
from jax import lax
from jax.experimental import pallas as pl
from jax.experimental.pallas import tpu as pltpu
from jax.sharding import Mesh
from jax.sharding import PartitionSpec as P

D = 8192
KV_HEADS = 8
GROUP = 8
HEAD_SIZE = 128
CHIP = ("grp", "tp_0", "tp_1")
CORE = "tp_2"
GRP_TP = CHIP + (CORE,)
CHIPS = 64
HALF = 4
LOW = -(2.0**100)
BF = jnp.bfloat16
F32 = jnp.float32


def swap(x):
    return lax.ppermute(x, CORE, [(0, 1), (1, 0)])


def exchange(x, axes):
    return lax.all_to_all(x, axes, split_axis=0, concat_axis=0, tiled=True)


def rounded(x):
    return lax.reduce_precision(x, 8, 7)


def by_core(core, mine, other, axis):
    first = jnp.concatenate([mine, other], axis)
    second = jnp.concatenate([other, mine], axis)
    return jnp.where(core == 0, first, second)


NT = (((1,), (1,)), ((), ()))
VMEM = pl.BlockSpec(memory_space=pltpu.VMEM)
SMEM = pl.BlockSpec(memory_space=pltpu.SMEM)


def call(kernel, shapes, specs, limit, cost, *operands):
    return pl.pallas_call(
        kernel,
        out_shape=shapes,
        in_specs=specs,
        out_specs=jax.tree.map(lambda _: VMEM, shapes),
        compiler_params=pltpu.CompilerParams(vmem_limit_bytes=limit * 2**20),
        cost_estimate=pl.CostEstimate(
            flops=cost, bytes_accessed=cost // 16, transcendentals=0
        ),
    )(*operands)


def load_kernel(x_ref, out_ref):
    out_ref[...] = x_ref[...]


def attend_kernel(core_ref, q_ref, k_ref, v_ref, kf_ref, vf_ref, ok_ref, pack_ref, out_ref):
    base = core_ref[0] * HALF
    row = lax.broadcasted_iota(jnp.int32, (256, 256), 0)
    col = lax.broadcasted_iota(jnp.int32, (256, 256), 1)
    valid = ((row % HALF) == (col // 64)) & (ok_ref[...] > 0)

    def both(near, far, kv):
        cols = slice(kv * HEAD_SIZE, (kv + 1) * HEAD_SIZE)
        parts = []
        for r in range(HALF):
            parts += [near[r, :, cols], far[base + r, :, cols]]
        return jnp.concatenate(parts, 0)

    s = jnp.concatenate(
        [
            lax.dot_general(
                q_ref[kv * 32 : (kv + 1) * 32, :],
                both(k_ref, kf_ref, kv),
                NT,
                preferred_element_type=F32,
            )
            for kv in range(KV_HEADS)
        ],
        0,
    )
    s = jnp.where(valid, s * (1.0 / math.sqrt(HEAD_SIZE)), LOW)
    top = jnp.max(s, 1, keepdims=True).astype(BF).astype(F32)
    p = jnp.where(valid, jnp.exp(s - top), 0.0)
    total = jnp.sum(p, 1, keepdims=True)
    p = p.astype(BF)
    total_hi = total.astype(BF).astype(F32)
    lane = lax.broadcasted_iota(jnp.int32, (256, 128), 1)
    stats = jnp.where(lane < 32, total_hi, total - total_hi)
    stats = jnp.where(lane < 16, top, stats)
    acc = jnp.concatenate(
        [
            jnp.dot(
                p[kv * 32 : (kv + 1) * 32],
                both(v_ref, vf_ref, kv),
                preferred_element_type=F32,
            )
            for kv in range(KV_HEADS)
        ],
        0,
    ).reshape(32, 8, 128)
    stats = jnp.where(lane.reshape(32, 8, 128) < 64, stats.reshape(32, 8, 128), pack_ref[...][None])
    upper = lax.broadcasted_iota(jnp.int32, (32, 8, 128), 1) < HALF
    even = jnp.where(upper, acc, pltpu.roll(stats, HALF, 1)).astype(BF)
    odd = jnp.where(upper, pltpu.roll(acc, HALF, 1), stats).astype(BF)
    for t in range(32):
        out_ref[2 * t] = even[t]
        out_ref[2 * t + 1] = odd[t]


def merge_kernel(at_ref, got_ref, q_ref, fk_ref, fv_ref, near_ref, far_ref):
    x = got_ref[...].astype(F32)
    stats = pltpu.roll(x, HALF, 1)
    tops = stats[:, :, 0:1]
    totals = stats[:, :, 16:17] + stats[:, :, 32:33]
    q = q_ref[...]
    scale = 1.0 / math.sqrt(HEAD_SIZE)
    s0 = jnp.sum(fk_ref[0] * q, 1, keepdims=True) * scale
    s1 = jnp.sum(fk_ref[1] * q, 1, keepdims=True) * scale
    second = at_ref[0] >= 1
    s1 = jnp.where(second, s1, LOW)
    peak = jnp.maximum(jnp.max(tops, 0), jnp.maximum(s0, s1))
    factor = jnp.exp(tops - peak[None])
    p0 = jnp.exp(s0 - peak)
    p1 = jnp.where(second, jnp.exp(s1 - peak), 0.0)
    below = jnp.sum(totals * factor, 0) + p0 + p1
    above = jnp.sum(x * factor, 0) + p0 * fv_ref[0] + p1 * fv_ref[1]
    row = lax.broadcasted_iota(jnp.int32, (8, 128), 0)
    attended = jnp.where(row < HALF, above / below, 0.0)
    turned = pltpu.roll(attended, 64, 1)
    first = at_ref[1] == 0
    near_ref[...] = jnp.where(first, attended, turned)[:HALF, :64].astype(BF)
    far_ref[...] = jnp.where(first, turned, attended)[:HALF, :64].astype(BF)


def state_kernel(got_ref, resid_ref, out_ref):
    state = jnp.sum(got_ref[...].astype(F32), 0) + resid_ref[...]
    out_ref[...] = jnp.broadcast_to(state.astype(BF)[None], out_ref.shape)


def head_kernel(u_ref, head_ref, action_ref, out_ref):
    u = jnp.concatenate([u_ref[i] for i in range(CHIPS)], 1)
    logits = lax.dot_general(head_ref[...], u, NT, preferred_element_type=F32)
    ids = lax.broadcasted_iota(jnp.int32, logits.shape, 0)
    high = jnp.max(logits, 0, keepdims=True)
    out_ref[...] = jnp.zeros_like(out_ref)
    out_ref[0:1, 0:8] = high
    out_ref[1:2, 0:8] = jnp.sum(jnp.exp(logits - high), 0, keepdims=True)
    out_ref[2:3, 0:8] = jnp.sum(
        jnp.where(ids == action_ref[...], logits, 0.0), 0, keepdims=True
    )


def pack_kernel(near_ref, far_ref, out_ref):
    a, b = near_ref[...], far_ref[...]
    high = jnp.maximum(a[0:1], b[0:1])
    total = a[1:2] * jnp.exp(a[0:1] - high) + b[1:2] * jnp.exp(b[0:1] - high)
    x = high + pltpu.roll(total, 8, 1) + pltpu.roll(a[2:3] + b[2:3], 16, 1)
    out_ref[...] = jnp.broadcast_to(x[None], out_ref.shape)


def final_kernel(start_ref, heard_ref, normed_ref, out_ref, normed_out):
    normed_out[...] = normed_ref[...][None]
    x = heard_ref[pl.ds(start_ref[0], CHIPS)]
    high = jnp.max(x, 0, keepdims=True)
    total = jnp.sum(pltpu.roll(x, 120, 2) * jnp.exp(x - high), 0)
    target = jnp.sum(pltpu.roll(x, 112, 2), 0)
    out_ref[...] = (target - high[0] - jnp.log(total))[:, 0:8]


def on_device(
    queries,
    step_token_keys,
    step_token_values,
    stored_key_cache,
    stored_value_cache,
    lengths,
    wo_sides,
    gain_sides,
    head,
    resid,
    actions,
):
    place = lax.axis_index(GRP_TP)
    chip = lax.axis_index(CHIP)
    core = lax.axis_index(CORE)
    side = lax.axis_index("role")
    step = 1 - side
    slots = stored_key_cache.shape[1]
    row0 = core * HALF

    def rows_of(x, start, axis=0):
        return lax.dynamic_slice_in_dim(x, start, HALF, axis)

    def chip_rows(x, far):
        near = rows_of(lax.dynamic_index_in_dim(x, step, 0, keepdims=False), row0)
        far = rows_of(lax.dynamic_index_in_dim(far, step, 0, keepdims=False), row0)
        return by_core(core, near, far, 1)

    spot = jnp.stack([step, core])
    q_half = chip_rows(queries, swap(queries))
    q_chip = jnp.pad(q_half.astype(F32), ((0, HALF), (0, 0)))
    sent = lax.optimization_barrier(
        jnp.broadcast_to(q_half[None], (CHIPS, *q_half.shape))
    )
    q = exchange(sent, CHIP).reshape(CHIPS * HALF, HEAD_SIZE)

    keys, values, gain, lengths, _ = lax.optimization_barrier(
        (stored_key_cache, stored_value_cache, gain_sides[0], lengths, sent)
    )
    keys_far, values_far = swap(keys), swap(values)
    keys, values = rows_of(keys, row0), rows_of(values, row0)
    gain_chip = by_core(core, gain, swap(gain), 0)

    lens = rows_of(lengths, row0)
    at = jnp.arange(slots, dtype=jnp.int32)
    position = jnp.concatenate([place * slots + at, (place + 1 - 2 * core) * slots + at])
    valid = (position[None, :] < lens[:, None]).astype(F32).reshape(1, 4 * 2 * slots)
    gain_hi = rounded(gain_chip)
    pack = jnp.concatenate([gain_hi, gain_chip - gain_hi]).reshape(HALF, 64)
    pack = jnp.concatenate([jnp.zeros_like(pack), pack], 1)
    pack = jnp.concatenate([pack, pack], 0)
    sent = call(
        attend_kernel,
        jax.ShapeDtypeStruct((CHIPS, 8, HEAD_SIZE), BF),
        [SMEM] + [VMEM] * 7,
        16,
        2 * 2 * 256 * 256 * 128,
        core[None],
        q,
        keys,
        values,
        keys_far,
        values_far,
        valid,
        pack,
    )
    got = exchange(sent, CHIP)
    w_side, resid, actions, new_keys, new_values, _ = lax.optimization_barrier(
        (wo_sides[0], resid, actions, step_token_keys, step_token_values, sent)
    )
    w_far = swap(w_side)
    w_mine = call(load_kernel, jax.ShapeDtypeStruct(w_side.shape, BF), [VMEM], 8, 1 << 20, w_side)
    r_chip = chip_rows(resid, swap(resid)).astype(F32)
    gains = got[:, HALF:, 64:].astype(F32).reshape(CHIPS, 2, HEAD_SIZE).sum(1)
    kv = chip // GROUP

    def fresh(x):
        x = lax.dynamic_slice(x, (0, row0, kv * HEAD_SIZE), (2, HALF, HEAD_SIZE))
        return jnp.pad(x.astype(F32), ((0, 0), (0, HALF), (0, 0)))

    part = jax.ShapeDtypeStruct((HALF, 64), BF)
    near, far = call(
        merge_kernel,
        (part, part),
        [SMEM] + [VMEM] * 4,
        16,
        CHIPS * 8 * HEAD_SIZE * 8,
        jnp.stack([step, core]),
        got,
        q_chip,
        fresh(new_keys),
        fresh(new_values),
    )
    share = jnp.dot(near, w_mine, preferred_element_type=F32)
    share = share + jnp.dot(far, w_far, preferred_element_type=F32)
    share = share.astype(BF).reshape(HALF, CHIPS, HEAD_SIZE).transpose(1, 0, 2)
    action = lax.dynamic_index_in_dim(actions, step, 0, keepdims=True)
    action = action - place * head.shape[1]
    share, gains, r_chip, action = lax.optimization_barrier((share, gains, r_chip, action))
    shares = exchange(share, CHIP)
    sent = call(
        state_kernel,
        jax.ShapeDtypeStruct((CHIPS, HALF, HEAD_SIZE), BF),
        [VMEM, VMEM],
        4,
        1 << 16,
        shares,
        r_chip,
    )
    mine = exchange(sent, CHIP)
    head_t, _ = lax.optimization_barrier((head.T, mine))
    head_t = call(load_kernel, jax.ShapeDtypeStruct(head_t.shape, BF), [VMEM], 24, 1 << 24, head_t)
    whole = by_core(core, mine, swap(mine), 1).astype(F32)
    square = jnp.sum(jnp.sum(whole * whole, 0), -1, keepdims=True)
    inverse = lax.rsqrt(square / D + 1e-05)
    normed = (whole * inverse[None] * gains[:, None, :]).astype(BF)
    own = lax.dynamic_index_in_dim(normed, chip, 0, keepdims=False)
    own = jnp.where(core == 0, own[:, :64], own[:, 64:])
    to_side = [(0, 1), (1, 0)]
    peer_normed = lax.ppermute(own, "role", to_side)
    width = head.shape[1]
    local = call(
        head_kernel,
        jax.ShapeDtypeStruct((8, 128), F32),
        [VMEM] * 3,
        24,
        2 * 8 * D * width,
        normed,
        head_t,
        action,
    )
    packed = call(
        pack_kernel,
        jax.ShapeDtypeStruct((2 * CHIPS, 1, HEAD_SIZE), F32),
        [VMEM, VMEM],
        4,
        1 << 16,
        local,
        swap(local),
    )
    heard = exchange(packed, ("role",) + CHIP)
    return call(
        final_kernel,
        (
            jax.ShapeDtypeStruct((1, 8), F32),
            jax.ShapeDtypeStruct((1, *peer_normed.shape), BF),
        ),
        [SMEM, VMEM, VMEM],
        4,
        1 << 16,
        ((1 - side) * CHIPS)[None],
        heard,
        peer_normed,
    )


def solution(mesh):
    split = Mesh(
        mesh.devices.reshape(mesh.shape["role"], mesh.shape["grp"], 4, 8, 2),
        ("role", "grp", "tp_0", "tp_1", "tp_2"),
    )
    return jax.shard_map(
        on_device,
        mesh=split,
        in_specs=(
            P(None, None, GRP_TP),
            P(),
            P(),
            P(None, GRP_TP, None),
            P(None, GRP_TP, None),
            P(),
            P("role", GRP_TP, None),
            P("role", GRP_TP),
            P(None, GRP_TP),
            P(None, None, GRP_TP),
            P(),
        ),
        out_specs=(P("role", None), P("role", None, GRP_TP)),
        check_vma=False,
    )
```

```python
import math

import jax
import jax.numpy as jnp
from jax import lax
from jax.experimental import pallas as pl
from jax.experimental.pallas import tpu as pltpu
from jax.sharding import Mesh
from jax.sharding import PartitionSpec as P

D = 8192
KV_HEADS = 8
GROUP = 8
HEAD_SIZE = 128
CHIP = ("grp", "tp_0", "tp_1")
CORE = "tp_2"
GRP_TP = CHIP + (CORE,)
CHIPS = 64
HALF = 4
LOW = -(2.0**100)
BF = jnp.bfloat16
F32 = jnp.float32


def swap(x):
    return lax.ppermute(x, CORE, [(0, 1), (1, 0)])


def exchange(x, axes):
    return lax.all_to_all(x, axes, split_axis=0, concat_axis=0, tiled=True)


def rounded(x):
    return lax.reduce_precision(x, 8, 7)


def by_core(core, mine, other, axis):
    first = jnp.concatenate([mine, other], axis)
    second = jnp.concatenate([other, mine], axis)
    return jnp.where(core == 0, first, second)


NT = (((1,), (1,)), ((), ()))
VMEM = pl.BlockSpec(memory_space=pltpu.VMEM)
SMEM = pl.BlockSpec(memory_space=pltpu.SMEM)


def call(kernel, shapes, specs, limit, cost, *operands):
    return pl.pallas_call(
        kernel,
        out_shape=shapes,
        in_specs=specs,
        out_specs=jax.tree.map(lambda _: VMEM, shapes),
        compiler_params=pltpu.CompilerParams(vmem_limit_bytes=limit * 2**20),
        cost_estimate=pl.CostEstimate(
            flops=cost, bytes_accessed=cost // 16, transcendentals=0
        ),
    )(*operands)


def load_kernel(x_ref, out_ref):
    out_ref[...] = x_ref[...]


def touch_kernel(x_ref, out_ref):
    out_ref[...] = x_ref[0:16, 0:128][0:8]


def attend_kernel(core_ref, q_ref, k_ref, v_ref, kf_ref, vf_ref, ok_ref, pack_ref, out_ref):
    base = core_ref[0] * HALF
    row = lax.broadcasted_iota(jnp.int32, (256, 256), 0)
    col = lax.broadcasted_iota(jnp.int32, (256, 256), 1)
    valid = ((row % HALF) == (col // 64)) & (ok_ref[...] > 0)

    def both(near, far, kv):
        cols = slice(kv * HEAD_SIZE, (kv + 1) * HEAD_SIZE)
        parts = []
        for r in range(HALF):
            parts += [near[r, :, cols], far[base + r, :, cols]]
        return jnp.concatenate(parts, 0)

    s = jnp.concatenate(
        [
            lax.dot_general(
                q_ref[kv * 32 : (kv + 1) * 32, :],
                both(k_ref, kf_ref, kv),
                NT,
                preferred_element_type=F32,
            )
            for kv in range(KV_HEADS)
        ],
        0,
    )
    s = jnp.where(valid, s * (1.0 / math.sqrt(HEAD_SIZE)), LOW)
    top = jnp.max(s, 1, keepdims=True).astype(BF).astype(F32)
    p = jnp.where(valid, jnp.exp(s - top), 0.0)
    total = jnp.sum(p, 1, keepdims=True)
    p = p.astype(BF)
    total_hi = total.astype(BF).astype(F32)
    lane = lax.broadcasted_iota(jnp.int32, (256, 128), 1)
    stats = jnp.where(lane < 32, total_hi, total - total_hi)
    stats = jnp.where(lane < 16, top, stats)
    acc = jnp.concatenate(
        [
            jnp.dot(
                p[kv * 32 : (kv + 1) * 32],
                both(v_ref, vf_ref, kv),
                preferred_element_type=F32,
            )
            for kv in range(KV_HEADS)
        ],
        0,
    ).reshape(32, 8, 128)
    stats = jnp.where(lane.reshape(32, 8, 128) < 64, stats.reshape(32, 8, 128), pack_ref[...][None])
    upper = lax.broadcasted_iota(jnp.int32, (32, 8, 128), 1) < HALF
    even = jnp.where(upper, acc, pltpu.roll(stats, HALF, 1)).astype(BF)
    odd = jnp.where(upper, pltpu.roll(acc, HALF, 1), stats).astype(BF)
    for t in range(32):
        out_ref[2 * t] = even[t]
        out_ref[2 * t + 1] = odd[t]


def merge_kernel(at_ref, got_ref, q_ref, fk_ref, fv_ref, near_ref, far_ref):
    x = got_ref[...].astype(F32)
    stats = pltpu.roll(x, HALF, 1)
    tops = stats[:, :, 0:1]
    totals = stats[:, :, 16:17] + stats[:, :, 32:33]
    q = q_ref[...]
    scale = 1.0 / math.sqrt(HEAD_SIZE)
    s0 = jnp.sum(fk_ref[0] * q, 1, keepdims=True) * scale
    s1 = jnp.sum(fk_ref[1] * q, 1, keepdims=True) * scale
    second = at_ref[0] >= 1
    s1 = jnp.where(second, s1, LOW)
    peak = jnp.maximum(jnp.max(tops, 0), jnp.maximum(s0, s1))
    factor = jnp.exp(tops - peak[None])
    p0 = jnp.exp(s0 - peak)
    p1 = jnp.where(second, jnp.exp(s1 - peak), 0.0)
    below = jnp.sum(totals * factor, 0) + p0 + p1
    above = jnp.sum(x * factor, 0) + p0 * fv_ref[0] + p1 * fv_ref[1]
    row = lax.broadcasted_iota(jnp.int32, (8, 128), 0)
    attended = jnp.where(row < HALF, above / below, 0.0)
    turned = pltpu.roll(attended, 64, 1)
    first = at_ref[1] == 0
    near_ref[...] = jnp.where(first, attended, turned)[:HALF, :64].astype(BF)
    far_ref[...] = jnp.where(first, turned, attended)[:HALF, :64].astype(BF)


def state_kernel(got_ref, resid_ref, out_ref):
    state = jnp.sum(got_ref[...].astype(F32), 0) + resid_ref[...]
    out_ref[...] = jnp.broadcast_to(state.astype(BF)[None], out_ref.shape)


def head_kernel(u_ref, head_ref, action_ref, touched_ref, out_ref):
    u = jnp.concatenate([u_ref[i] for i in range(CHIPS)], 1)
    logits = lax.dot_general(head_ref[...], u, NT, preferred_element_type=F32)
    ids = lax.broadcasted_iota(jnp.int32, logits.shape, 0)
    high = jnp.max(logits, 0, keepdims=True)
    out_ref[...] = jnp.zeros_like(out_ref)
    out_ref[0:1, 0:8] = high
    out_ref[1:2, 0:8] = jnp.sum(jnp.exp(logits - high), 0, keepdims=True)
    out_ref[2:3, 0:8] = jnp.sum(
        jnp.where(ids == action_ref[...], logits, 0.0), 0, keepdims=True
    )


def pack_kernel(near_ref, far_ref, out_ref):
    a, b = near_ref[...], far_ref[...]
    high = jnp.maximum(a[0:1], b[0:1])
    total = a[1:2] * jnp.exp(a[0:1] - high) + b[1:2] * jnp.exp(b[0:1] - high)
    x = high + pltpu.roll(total, 8, 1) + pltpu.roll(a[2:3] + b[2:3], 16, 1)
    out_ref[...] = jnp.broadcast_to(x[None], out_ref.shape)


def final_kernel(start_ref, heard_ref, normed_ref, out_ref, normed_out):
    normed_out[...] = normed_ref[...][None]
    x = heard_ref[pl.ds(start_ref[0], CHIPS)]
    high = jnp.max(x, 0, keepdims=True)
    total = jnp.sum(pltpu.roll(x, 120, 2) * jnp.exp(x - high), 0)
    target = jnp.sum(pltpu.roll(x, 112, 2), 0)
    out_ref[...] = (target - high[0] - jnp.log(total))[:, 0:8]


def on_device(
    queries,
    step_token_keys,
    step_token_values,
    stored_key_cache,
    stored_value_cache,
    lengths,
    wo_sides,
    gain_sides,
    head,
    resid,
    actions,
):
    place = lax.axis_index(GRP_TP)
    chip = lax.axis_index(CHIP)
    core = lax.axis_index(CORE)
    side = lax.axis_index("role")
    step = 1 - side
    slots = stored_key_cache.shape[1]
    row0 = core * HALF

    def rows_of(x, start, axis=0):
        return lax.dynamic_slice_in_dim(x, start, HALF, axis)

    def chip_rows(x, far):
        near = rows_of(lax.dynamic_index_in_dim(x, step, 0, keepdims=False), row0)
        far = rows_of(lax.dynamic_index_in_dim(far, step, 0, keepdims=False), row0)
        return by_core(core, near, far, 1)

    spot = jnp.stack([step, core])
    q_half = chip_rows(queries, swap(queries))
    q_chip = jnp.pad(q_half.astype(F32), ((0, HALF), (0, 0)))
    sent = lax.optimization_barrier(
        jnp.broadcast_to(q_half[None], (CHIPS, *q_half.shape))
    )
    q = exchange(sent, CHIP).reshape(CHIPS * HALF, HEAD_SIZE)

    keys, values, gain, gain_far, _ = lax.optimization_barrier(
        (stored_key_cache, stored_value_cache, gain_sides, swap(gain_sides), sent)
    )
    keys_far, values_far = swap(keys), swap(values)
    keys, values = rows_of(keys, row0), rows_of(values, row0)
    gain_chip = by_core(core, gain, gain_far, 0)

    lens = rows_of(lengths, row0)
    at = jnp.arange(slots, dtype=jnp.int32)
    position = jnp.concatenate([place * slots + at, (place + 1 - 2 * core) * slots + at])
    valid = (position[None, :] < lens[:, None]).astype(F32).reshape(1, 4 * 2 * slots)
    gain_hi = rounded(gain_chip)
    pack = jnp.concatenate([gain_hi, gain_chip - gain_hi])
    pack = jnp.concatenate([jnp.zeros_like(pack), pack], 1)
    pack = jnp.concatenate([pack, pack], 0)
    sent = call(
        attend_kernel,
        jax.ShapeDtypeStruct((CHIPS, 8, HEAD_SIZE), BF),
        [SMEM] + [VMEM] * 7,
        16,
        2 * 2 * 256 * 256 * 128,
        core[None],
        q,
        keys,
        values,
        keys_far,
        values_far,
        valid,
        pack,
    )
    got = exchange(sent, CHIP)
    w_side, resid, actions, new_keys, new_values, _ = lax.optimization_barrier(
        (wo_sides[0], resid, actions, step_token_keys, step_token_values, sent)
    )
    w_far = swap(w_side)
    w_mine = call(load_kernel, jax.ShapeDtypeStruct(w_side.shape, BF), [VMEM], 8, 1 << 20, w_side)
    r_chip = chip_rows(resid, swap(resid)).astype(F32)
    kv = chip // GROUP

    def fresh(x):
        x = lax.dynamic_slice(x, (0, row0, kv * HEAD_SIZE), (2, HALF, HEAD_SIZE))
        return jnp.pad(x.astype(F32), ((0, 0), (0, HALF), (0, 0)))

    part = jax.ShapeDtypeStruct((HALF, 64), BF)
    near, far = call(
        merge_kernel,
        (part, part),
        [SMEM] + [VMEM] * 4,
        16,
        CHIPS * 8 * HEAD_SIZE * 8,
        jnp.stack([step, core]),
        got,
        q_chip,
        fresh(new_keys),
        fresh(new_values),
    )
    share = jnp.dot(near, w_mine, preferred_element_type=F32)
    share = share + jnp.dot(far, w_far, preferred_element_type=F32)
    share = share.astype(BF).reshape(HALF, CHIPS, HEAD_SIZE).transpose(1, 0, 2)
    action = lax.dynamic_index_in_dim(actions, step, 0, keepdims=True)
    action = action - place * head.shape[1]
    share, r_chip, action = lax.optimization_barrier((share, r_chip, action))
    shares = exchange(share, CHIP)
    sent = call(
        state_kernel,
        jax.ShapeDtypeStruct((CHIPS, HALF, HEAD_SIZE), BF),
        [VMEM, VMEM],
        4,
        1 << 16,
        shares,
        r_chip,
    )
    mine = exchange(sent, CHIP)
    head_t, got, _ = lax.optimization_barrier((head.T, got, mine))
    touched = call(touch_kernel, jax.ShapeDtypeStruct((8, 128), BF), [VMEM], 24, 1 << 24, head_t)
    gains = got[:, HALF:, 64:].astype(F32).reshape(CHIPS, 2, HEAD_SIZE).sum(1)
    whole = by_core(core, mine, swap(mine), 1).astype(F32)
    square = jnp.sum(jnp.sum(whole * whole, 0), -1, keepdims=True)
    inverse = lax.rsqrt(square / D + 1e-05)
    normed = (whole * inverse[None] * gains[:, None, :]).astype(BF)
    own = lax.dynamic_index_in_dim(normed, chip, 0, keepdims=False)
    own = jnp.where(core == 0, own[:, :64], own[:, 64:])
    to_side = [(0, 1), (1, 0)]
    peer_normed = lax.ppermute(own, "role", to_side)
    width = head.shape[1]
    local = call(
        head_kernel,
        jax.ShapeDtypeStruct((8, 128), F32),
        [VMEM] * 4,
        24,
        2 * 8 * D * width,
        normed,
        head_t,
        action,
        touched,
    )
    packed = call(
        pack_kernel,
        jax.ShapeDtypeStruct((2 * CHIPS, 1, HEAD_SIZE), F32),
        [VMEM, VMEM],
        4,
        1 << 16,
        local,
        swap(local),
    )
    heard = exchange(packed, ("role",) + CHIP)
    return call(
        final_kernel,
        (
            jax.ShapeDtypeStruct((1, 8), F32),
            jax.ShapeDtypeStruct((1, *peer_normed.shape), BF),
        ),
        [SMEM, VMEM, VMEM],
        4,
        1 << 16,
        ((1 - side) * CHIPS)[None],
        heard,
        peer_normed,
    )


def solution(mesh):
    split = Mesh(
        mesh.devices.reshape(mesh.shape["role"], mesh.shape["grp"], 4, 8, 2),
        ("role", "grp", "tp_0", "tp_1", "tp_2"),
    )
    return jax.shard_map(
        on_device,
        mesh=split,
        in_specs=(
            P(None, None, GRP_TP),
            P(),
            P(),
            P(None, GRP_TP, None),
            P(None, GRP_TP, None),
            P(),
            P("role", GRP_TP, None),
            P("role", GRP_TP),
            P(None, GRP_TP),
            P(None, None, GRP_TP),
            P(),
        ),
        out_specs=(P("role", None), P("role", None, GRP_TP)),
        check_vma=False,
    )
```

```python
import math

import jax
import jax.numpy as jnp
from jax import lax
from jax.experimental import pallas as pl
from jax.experimental.pallas import tpu as pltpu
from jax.sharding import Mesh
from jax.sharding import PartitionSpec as P

D = 8192
KV_HEADS = 8
GROUP = 8
HEAD_SIZE = 128
CHIP = ("grp", "tp_0", "tp_1")
CORE = "tp_2"
GRP_TP = CHIP + (CORE,)
CHIPS = 64
HALF = 4
LOW = -(2.0**100)
BF = jnp.bfloat16
F32 = jnp.float32


def swap(x):
    return lax.ppermute(x, CORE, [(0, 1), (1, 0)])


def exchange(x, axes):
    return lax.all_to_all(x, axes, split_axis=0, concat_axis=0, tiled=True)


def rounded(x):
    return lax.reduce_precision(x, 8, 7)


def by_core(core, mine, other, axis):
    first = jnp.concatenate([mine, other], axis)
    second = jnp.concatenate([other, mine], axis)
    return jnp.where(core == 0, first, second)


NT = (((1,), (1,)), ((), ()))
VMEM = pl.BlockSpec(memory_space=pltpu.VMEM)
SMEM = pl.BlockSpec(memory_space=pltpu.SMEM)


def call(kernel, shapes, specs, limit, cost, *operands, scratch=()):
    return pl.pallas_call(
        kernel,
        out_shape=shapes,
        in_specs=specs,
        scratch_shapes=scratch,
        out_specs=jax.tree.map(lambda _: VMEM, shapes),
        compiler_params=pltpu.CompilerParams(vmem_limit_bytes=limit * 2**20),
        cost_estimate=pl.CostEstimate(
            flops=cost, bytes_accessed=cost // 16, transcendentals=0
        ),
    )(*operands)


def load_kernel(x_ref, out_ref):
    out_ref[...] = x_ref[...]


def touch_kernel(x_ref, out_ref):
    out_ref[...] = x_ref[0:16, 0:128][0:8]


def attend_kernel(core_ref, q_ref, k_ref, v_ref, kf_ref, vf_ref, ok_ref, pack_ref, out_ref):
    base = core_ref[0] * HALF
    row = lax.broadcasted_iota(jnp.int32, (256, 256), 0)
    col = lax.broadcasted_iota(jnp.int32, (256, 256), 1)
    valid = ((row % HALF) == (col // 64)) & (ok_ref[...] > 0)

    def both(near, far, kv):
        cols = slice(kv * HEAD_SIZE, (kv + 1) * HEAD_SIZE)
        parts = []
        for r in range(HALF):
            parts += [near[r, :, cols], far[base + r, :, cols]]
        return jnp.concatenate(parts, 0)

    s = jnp.concatenate(
        [
            lax.dot_general(
                q_ref[kv * 32 : (kv + 1) * 32, :],
                both(k_ref, kf_ref, kv),
                NT,
                preferred_element_type=F32,
            )
            for kv in range(KV_HEADS)
        ],
        0,
    )
    s = jnp.where(valid, s * (1.0 / math.sqrt(HEAD_SIZE)), LOW)
    top = jnp.max(s, 1, keepdims=True).astype(BF).astype(F32)
    p = jnp.where(valid, jnp.exp(s - top), 0.0)
    total = jnp.sum(p, 1, keepdims=True)
    p = p.astype(BF)
    total_hi = total.astype(BF).astype(F32)
    lane = lax.broadcasted_iota(jnp.int32, (256, 128), 1)
    stats = jnp.where(lane < 32, total_hi, total - total_hi)
    stats = jnp.where(lane < 16, top, stats)
    acc = jnp.concatenate(
        [
            jnp.dot(
                p[kv * 32 : (kv + 1) * 32],
                both(v_ref, vf_ref, kv),
                preferred_element_type=F32,
            )
            for kv in range(KV_HEADS)
        ],
        0,
    ).reshape(32, 8, 128)
    stats = jnp.where(lane.reshape(32, 8, 128) < 64, stats.reshape(32, 8, 128), pack_ref[...][None])
    upper = lax.broadcasted_iota(jnp.int32, (32, 8, 128), 1) < HALF
    even = jnp.where(upper, acc, pltpu.roll(stats, HALF, 1)).astype(BF)
    odd = jnp.where(upper, pltpu.roll(acc, HALF, 1), stats).astype(BF)
    for t in range(32):
        out_ref[2 * t] = even[t]
        out_ref[2 * t + 1] = odd[t]


def merge_kernel(step_ref, core_ref, got_ref, q_ref, fk_ref, fv_ref, near_ref, far_ref):
    x = got_ref[...].astype(F32)
    stats = pltpu.roll(x, HALF, 1)
    tops = stats[:, :, 0:1]
    totals = stats[:, :, 16:17] + stats[:, :, 32:33]
    q = q_ref[...]
    scale = 1.0 / math.sqrt(HEAD_SIZE)
    s0 = jnp.sum(fk_ref[0] * q, 1, keepdims=True) * scale
    s1 = jnp.sum(fk_ref[1] * q, 1, keepdims=True) * scale
    second = step_ref[0] >= 1
    s1 = jnp.where(second, s1, LOW)
    peak = jnp.maximum(jnp.max(tops, 0), jnp.maximum(s0, s1))
    factor = jnp.exp(tops - peak[None])
    p0 = jnp.exp(s0 - peak)
    p1 = jnp.where(second, jnp.exp(s1 - peak), 0.0)
    below = jnp.sum(totals * factor, 0) + p0 + p1
    above = jnp.sum(x * factor, 0) + p0 * fv_ref[0] + p1 * fv_ref[1]
    row = lax.broadcasted_iota(jnp.int32, (8, 128), 0)
    attended = jnp.where(row < HALF, above / below, 0.0)
    turned = pltpu.roll(attended, 64, 1)
    first = core_ref[0] == 0
    near_ref[...] = jnp.where(first, attended, turned)[:HALF, :64].astype(BF)
    far_ref[...] = jnp.where(first, turned, attended)[:HALF, :64].astype(BF)


def state_kernel(got_ref, resid_ref, out_ref):
    state = jnp.sum(got_ref[...].astype(F32), 0) + resid_ref[...]
    out_ref[...] = jnp.broadcast_to(state.astype(BF)[None], out_ref.shape)


def head_kernel(
    core_ref, chip_ref, near_ref, far_ref, got_ref, head_ref, action_ref, touched_ref, out_ref, own_ref, u_ref
):
    near, far = near_ref[...].astype(F32), far_ref[...].astype(F32)
    first = core_ref[0] == 0
    whole = jnp.concatenate([jnp.where(first, near, far), jnp.where(first, far, near)], 1)
    square = jnp.sum(jnp.sum(whole * whole, 0), 1, keepdims=True)
    inverse = lax.rsqrt(square / D + 1e-05)
    gain = got_ref[...].astype(F32)
    gain = gain + pltpu.roll(gain, 6, 1)
    left = lax.broadcasted_iota(jnp.int32, (CHIPS, 1, HEAD_SIZE), 2) < 64
    gain = jnp.where(left, pltpu.roll(gain[:, 4:5], 64, 2), gain[:, 5:6])
    u_ref[...] = (whole * inverse[None] * gain).astype(BF)
    own_ref[...] = u_ref[chip_ref[0]]
    u = jnp.concatenate([u_ref[i] for i in range(CHIPS)], 1)
    logits = lax.dot_general(head_ref[...], u, NT, preferred_element_type=F32)
    ids = lax.broadcasted_iota(jnp.int32, logits.shape, 0)
    high = jnp.max(logits, 0, keepdims=True)
    out_ref[...] = jnp.zeros_like(out_ref)
    out_ref[0:1, 0:8] = high
    out_ref[1:2, 0:8] = jnp.sum(jnp.exp(logits - high), 0, keepdims=True)
    out_ref[2:3, 0:8] = jnp.sum(
        jnp.where(ids == action_ref[...], logits, 0.0), 0, keepdims=True
    )


def pack_kernel(near_ref, far_ref, out_ref):
    a, b = near_ref[...], far_ref[...]
    high = jnp.maximum(a[0:1], b[0:1])
    total = a[1:2] * jnp.exp(a[0:1] - high) + b[1:2] * jnp.exp(b[0:1] - high)
    x = high + pltpu.roll(total, 8, 1) + pltpu.roll(a[2:3] + b[2:3], 16, 1)
    out_ref[...] = jnp.broadcast_to(x[None], out_ref.shape)


def final_kernel(start_ref, heard_ref, normed_ref, out_ref, normed_out):
    normed_out[...] = normed_ref[...][None]
    x = heard_ref[pl.ds(start_ref[0], CHIPS)]
    high = jnp.max(x, 0, keepdims=True)
    total = jnp.sum(pltpu.roll(x, 120, 2) * jnp.exp(x - high), 0)
    target = jnp.sum(pltpu.roll(x, 112, 2), 0)
    out_ref[...] = (target - high[0] - jnp.log(total))[:, 0:8]


def on_device(
    queries,
    step_token_keys,
    step_token_values,
    stored_key_cache,
    stored_value_cache,
    lengths,
    wo_sides,
    gain_sides,
    head,
    resid,
    actions,
):
    place = lax.axis_index(GRP_TP)
    chip = lax.axis_index(CHIP)
    core = lax.axis_index(CORE)
    side = lax.axis_index("role")
    step = 1 - side
    slots = stored_key_cache.shape[1]
    row0 = core * HALF

    def rows_of(x, start, axis=0):
        return lax.dynamic_slice_in_dim(x, start, HALF, axis)

    def chip_rows(x, far):
        near = rows_of(lax.dynamic_index_in_dim(x, step, 0, keepdims=False), row0)
        far = rows_of(lax.dynamic_index_in_dim(far, step, 0, keepdims=False), row0)
        return by_core(core, near, far, 1)

    spot = jnp.stack([step, core])
    q_half = chip_rows(queries, swap(queries))
    q_chip = jnp.pad(q_half.astype(F32), ((0, HALF), (0, 0)))
    sent = lax.optimization_barrier(
        jnp.broadcast_to(q_half[None], (CHIPS, *q_half.shape))
    )
    q = exchange(sent, CHIP).reshape(CHIPS * HALF, HEAD_SIZE)

    keys, values, lengths, gain, gain_far, _ = lax.optimization_barrier(
        (stored_key_cache, stored_value_cache, lengths, gain_sides, swap(gain_sides), sent)
    )
    keys_far, values_far = swap(keys), swap(values)
    keys, values = rows_of(keys, row0), rows_of(values, row0)
    gain_chip = by_core(core, gain, gain_far, 0)

    lens = rows_of(lengths, row0)
    at = jnp.arange(slots, dtype=jnp.int32)
    position = jnp.concatenate([place * slots + at, (place + 1 - 2 * core) * slots + at])
    valid = (position[None, :] < lens[:, None]).astype(F32).reshape(1, 4 * 2 * slots)
    gain_hi = rounded(gain_chip)
    pack = jnp.concatenate([gain_hi, gain_chip - gain_hi])
    pack = jnp.concatenate([jnp.zeros_like(pack), pack], 1)
    pack = jnp.concatenate([pack, pack], 0)
    sent = call(
        attend_kernel,
        jax.ShapeDtypeStruct((CHIPS, 8, HEAD_SIZE), BF),
        [SMEM] + [VMEM] * 7,
        16,
        2 * 2 * 256 * 256 * 128,
        core[None],
        q,
        keys,
        values,
        keys_far,
        values_far,
        valid,
        pack,
    )
    got = exchange(sent, CHIP)
    w_side, resid, actions, new_keys, new_values, _ = lax.optimization_barrier(
        (wo_sides[0], resid, actions, step_token_keys, step_token_values, sent)
    )
    w_far = swap(w_side)
    w_mine = call(load_kernel, jax.ShapeDtypeStruct(w_side.shape, BF), [VMEM], 8, 1 << 20, w_side)
    r_chip = chip_rows(resid, swap(resid)).astype(F32)
    kv = chip // GROUP

    def fresh(x):
        x = lax.dynamic_slice(x, (0, row0, kv * HEAD_SIZE), (2, HALF, HEAD_SIZE))
        return jnp.pad(x.astype(F32), ((0, 0), (0, HALF), (0, 0)))

    part = jax.ShapeDtypeStruct((HALF, 64), BF)
    near, far = call(
        merge_kernel,
        (part, part),
        [SMEM] * 2 + [VMEM] * 4,
        16,
        CHIPS * 8 * HEAD_SIZE * 8,
        step[None],
        core[None],
        got,
        q_chip,
        fresh(new_keys),
        fresh(new_values),
    )
    share = jnp.dot(near, w_mine, preferred_element_type=F32)
    share = share + jnp.dot(far, w_far, preferred_element_type=F32)
    share = share.astype(BF).reshape(HALF, CHIPS, HEAD_SIZE).transpose(1, 0, 2)
    action = lax.dynamic_index_in_dim(actions, step, 0, keepdims=True)
    action = action - place * head.shape[1]
    share, r_chip, action = lax.optimization_barrier((share, r_chip, action))
    shares = exchange(share, CHIP)
    sent = call(
        state_kernel,
        jax.ShapeDtypeStruct((CHIPS, HALF, HEAD_SIZE), BF),
        [VMEM, VMEM],
        4,
        1 << 16,
        shares,
        r_chip,
    )
    mine = exchange(sent, CHIP)
    head_t, _ = lax.optimization_barrier((head.T, mine))
    touched = call(touch_kernel, jax.ShapeDtypeStruct((8, 128), BF), [VMEM], 24, 1 << 24, head_t)
    local, own = call(
        head_kernel,
        (jax.ShapeDtypeStruct((8, 128), F32), jax.ShapeDtypeStruct((8, HEAD_SIZE), BF)),
        [SMEM] * 2 + [VMEM] * 6,
        24,
        2 * 8 * D * head.shape[1],
        core[None],
        chip[None],
        mine,
        swap(mine),
        got,
        head_t,
        action,
        touched,
        scratch=[pltpu.VMEM((CHIPS, 8, HEAD_SIZE), BF)],
    )
    own = jnp.where(core == 0, own[:, :64], own[:, 64:])
    peer_normed = lax.ppermute(own, "role", [(0, 1), (1, 0)])
    packed = call(
        pack_kernel,
        jax.ShapeDtypeStruct((2 * CHIPS, 1, HEAD_SIZE), F32),
        [VMEM, VMEM],
        4,
        1 << 16,
        local,
        swap(local),
    )
    heard = exchange(packed, ("role",) + CHIP)
    return call(
        final_kernel,
        (
            jax.ShapeDtypeStruct((1, 8), F32),
            jax.ShapeDtypeStruct((1, *peer_normed.shape), BF),
        ),
        [SMEM, VMEM, VMEM],
        4,
        1 << 16,
        ((1 - side) * CHIPS)[None],
        heard,
        peer_normed,
    )


def solution(mesh):
    split = Mesh(
        mesh.devices.reshape(mesh.shape["role"], mesh.shape["grp"], 4, 8, 2),
        ("role", "grp", "tp_0", "tp_1", "tp_2"),
    )
    return jax.shard_map(
        on_device,
        mesh=split,
        in_specs=(
            P(None, None, GRP_TP),
            P(),
            P(),
            P(None, GRP_TP, None),
            P(None, GRP_TP, None),
            P(),
            P("role", GRP_TP, None),
            P("role", GRP_TP),
            P(None, GRP_TP),
            P(None, None, GRP_TP),
            P(),
        ),
        out_specs=(P("role", None), P("role", None, GRP_TP)),
        check_vma=False,
    )
```

```python
import math

import jax
import jax.numpy as jnp
from jax import lax
from jax.experimental import pallas as pl
from jax.experimental.pallas import tpu as pltpu
from jax.sharding import Mesh
from jax.sharding import PartitionSpec as P

D = 8192
KV_HEADS = 8
GROUP = 8
HEAD_SIZE = 128
CHIP = ("grp", "tp_0", "tp_1")
CORE = "tp_2"
GRP_TP = CHIP + (CORE,)
CHIPS = 64
HALF = 4
LOW = -(2.0**100)
BF = jnp.bfloat16
F32 = jnp.float32


def swap(x):
    return lax.ppermute(x, CORE, [(0, 1), (1, 0)])


def exchange(x, axes):
    return lax.all_to_all(x, axes, split_axis=0, concat_axis=0, tiled=True)


def rounded(x):
    return lax.reduce_precision(x, 8, 7)


def by_core(core, mine, other, axis):
    first = jnp.concatenate([mine, other], axis)
    second = jnp.concatenate([other, mine], axis)
    return jnp.where(core == 0, first, second)


NT = (((1,), (1,)), ((), ()))
VMEM = pl.BlockSpec(memory_space=pltpu.VMEM)
SMEM = pl.BlockSpec(memory_space=pltpu.SMEM)


def call(kernel, shapes, specs, limit, cost, *operands, scratch=()):
    return pl.pallas_call(
        kernel,
        out_shape=shapes,
        in_specs=specs,
        scratch_shapes=scratch,
        out_specs=jax.tree.map(lambda _: VMEM, shapes),
        compiler_params=pltpu.CompilerParams(vmem_limit_bytes=limit * 2**20),
        cost_estimate=pl.CostEstimate(
            flops=cost, bytes_accessed=cost // 16, transcendentals=0
        ),
    )(*operands)


def load_kernel(x_ref, out_ref):
    out_ref[...] = x_ref[...]


def attend_kernel(core_ref, q_ref, k_ref, v_ref, kf_ref, vf_ref, ok_ref, pack_ref, out_ref):
    base = core_ref[0] * HALF
    row = lax.broadcasted_iota(jnp.int32, (256, 256), 0)
    col = lax.broadcasted_iota(jnp.int32, (256, 256), 1)
    valid = ((row % HALF) == (col // 64)) & (ok_ref[...] > 0)

    def both(near, far, kv):
        cols = slice(kv * HEAD_SIZE, (kv + 1) * HEAD_SIZE)
        parts = []
        for r in range(HALF):
            parts += [near[r, :, cols], far[base + r, :, cols]]
        return jnp.concatenate(parts, 0)

    s = jnp.concatenate(
        [
            lax.dot_general(
                q_ref[kv * 32 : (kv + 1) * 32, :],
                both(k_ref, kf_ref, kv),
                NT,
                preferred_element_type=F32,
            )
            for kv in range(KV_HEADS)
        ],
        0,
    )
    s = jnp.where(valid, s * (1.0 / math.sqrt(HEAD_SIZE)), LOW)
    top = jnp.max(s, 1, keepdims=True).astype(BF).astype(F32)
    p = jnp.where(valid, jnp.exp(s - top), 0.0)
    total = jnp.sum(p, 1, keepdims=True)
    p = p.astype(BF)
    total_hi = total.astype(BF).astype(F32)
    lane = lax.broadcasted_iota(jnp.int32, (256, 128), 1)
    stats = jnp.where(lane < 32, total_hi, total - total_hi)
    stats = jnp.where(lane < 16, top, stats)
    acc = jnp.concatenate(
        [
            jnp.dot(
                p[kv * 32 : (kv + 1) * 32],
                both(v_ref, vf_ref, kv),
                preferred_element_type=F32,
            )
            for kv in range(KV_HEADS)
        ],
        0,
    ).reshape(32, 8, 128)
    stats = jnp.where(lane.reshape(32, 8, 128) < 64, stats.reshape(32, 8, 128), pack_ref[...][None])
    upper = lax.broadcasted_iota(jnp.int32, (32, 8, 128), 1) < HALF
    even = jnp.where(upper, acc, pltpu.roll(stats, HALF, 1)).astype(BF)
    odd = jnp.where(upper, pltpu.roll(acc, HALF, 1), stats).astype(BF)
    for t in range(32):
        out_ref[2 * t] = even[t]
        out_ref[2 * t + 1] = odd[t]


def merge_kernel(step_ref, core_ref, got_ref, q_ref, fk_ref, fv_ref, near_ref, far_ref):
    x = got_ref[...].astype(F32)
    stats = pltpu.roll(x, HALF, 1)
    tops = stats[:, :, 0:1]
    totals = stats[:, :, 16:17] + stats[:, :, 32:33]
    q = q_ref[...]
    scale = 1.0 / math.sqrt(HEAD_SIZE)
    s0 = jnp.sum(fk_ref[0] * q, 1, keepdims=True) * scale
    s1 = jnp.sum(fk_ref[1] * q, 1, keepdims=True) * scale
    second = step_ref[0] >= 1
    s1 = jnp.where(second, s1, LOW)
    peak = jnp.maximum(jnp.max(tops, 0), jnp.maximum(s0, s1))
    factor = jnp.exp(tops - peak[None])
    p0 = jnp.exp(s0 - peak)
    p1 = jnp.where(second, jnp.exp(s1 - peak), 0.0)
    below = jnp.sum(totals * factor, 0) + p0 + p1
    above = jnp.sum(x * factor, 0) + p0 * fv_ref[0] + p1 * fv_ref[1]
    row = lax.broadcasted_iota(jnp.int32, (8, 128), 0)
    attended = jnp.where(row < HALF, above / below, 0.0)
    turned = pltpu.roll(attended, 64, 1)
    first = core_ref[0] == 0
    near_ref[...] = jnp.where(first, attended, turned)[:HALF, :64].astype(BF)
    far_ref[...] = jnp.where(first, turned, attended)[:HALF, :64].astype(BF)


def state_kernel(got_ref, resid_ref, out_ref):
    state = jnp.sum(got_ref[...].astype(F32), 0) + resid_ref[...]
    out_ref[...] = jnp.broadcast_to(state.astype(BF)[None], out_ref.shape)


def head_kernel(
    core_ref, chip_ref, near_ref, far_ref, got_ref, head_ref, action_ref, out_ref, own_ref, u_ref
):
    near, far = near_ref[...].astype(F32), far_ref[...].astype(F32)
    first = core_ref[0] == 0
    whole = jnp.concatenate([jnp.where(first, near, far), jnp.where(first, far, near)], 1)
    square = jnp.sum(jnp.sum(whole * whole, 0), 1, keepdims=True)
    inverse = lax.rsqrt(square / D + 1e-05)
    gain = got_ref[...].astype(F32)
    gain = gain + pltpu.roll(gain, 6, 1)
    left = lax.broadcasted_iota(jnp.int32, (CHIPS, 1, HEAD_SIZE), 2) < 64
    gain = jnp.where(left, pltpu.roll(gain[:, 4:5], 64, 2), gain[:, 5:6])
    u_ref[...] = (whole * inverse[None] * gain).astype(BF)
    own_ref[...] = u_ref[chip_ref[0]]
    u = jnp.concatenate([u_ref[i] for i in range(CHIPS)], 1)
    logits = lax.dot_general(head_ref[...], u, NT, preferred_element_type=F32)
    ids = lax.broadcasted_iota(jnp.int32, logits.shape, 0)
    high = jnp.max(logits, 0, keepdims=True)
    out_ref[...] = jnp.zeros_like(out_ref)
    out_ref[0:1, 0:8] = high
    out_ref[1:2, 0:8] = jnp.sum(jnp.exp(logits - high), 0, keepdims=True)
    out_ref[2:3, 0:8] = jnp.sum(
        jnp.where(ids == action_ref[...], logits, 0.0), 0, keepdims=True
    )


def pack_kernel(near_ref, far_ref, out_ref):
    a, b = near_ref[...], far_ref[...]
    high = jnp.maximum(a[0:1], b[0:1])
    total = a[1:2] * jnp.exp(a[0:1] - high) + b[1:2] * jnp.exp(b[0:1] - high)
    x = high + pltpu.roll(total, 8, 1) + pltpu.roll(a[2:3] + b[2:3], 16, 1)
    out_ref[...] = jnp.broadcast_to(x[None], out_ref.shape)


def final_kernel(start_ref, heard_ref, normed_ref, out_ref, normed_out):
    normed_out[...] = normed_ref[...][None]
    x = heard_ref[pl.ds(start_ref[0], CHIPS)]
    high = jnp.max(x, 0, keepdims=True)
    total = jnp.sum(pltpu.roll(x, 120, 2) * jnp.exp(x - high), 0)
    target = jnp.sum(pltpu.roll(x, 112, 2), 0)
    out_ref[...] = (target - high[0] - jnp.log(total))[:, 0:8]


def on_device(
    queries,
    step_token_keys,
    step_token_values,
    stored_key_cache,
    stored_value_cache,
    lengths,
    wo_sides,
    gain_sides,
    head,
    resid,
    actions,
):
    place = lax.axis_index(GRP_TP)
    chip = lax.axis_index(CHIP)
    core = lax.axis_index(CORE)
    side = lax.axis_index("role")
    step = 1 - side
    slots = stored_key_cache.shape[1]
    row0 = core * HALF

    def rows_of(x, start, axis=0):
        return lax.dynamic_slice_in_dim(x, start, HALF, axis)

    def chip_rows(x, far):
        near = rows_of(lax.dynamic_index_in_dim(x, step, 0, keepdims=False), row0)
        far = rows_of(lax.dynamic_index_in_dim(far, step, 0, keepdims=False), row0)
        return by_core(core, near, far, 1)

    spot = jnp.stack([step, core])
    q_half = chip_rows(queries, swap(queries))
    q_chip = jnp.pad(q_half.astype(F32), ((0, HALF), (0, 0)))
    sent = lax.optimization_barrier(
        jnp.broadcast_to(q_half[None], (CHIPS, *q_half.shape))
    )
    q = exchange(sent, CHIP).reshape(CHIPS * HALF, HEAD_SIZE)

    keys, values, lengths, gain, gain_far, _ = lax.optimization_barrier(
        (stored_key_cache, stored_value_cache, lengths, gain_sides, swap(gain_sides), sent)
    )
    keys_far, values_far = swap(keys), swap(values)
    keys, values = rows_of(keys, row0), rows_of(values, row0)
    gain_chip = by_core(core, gain, gain_far, 0)

    lens = rows_of(lengths, row0)
    at = jnp.arange(slots, dtype=jnp.int32)
    position = jnp.concatenate([place * slots + at, (place + 1 - 2 * core) * slots + at])
    valid = (position[None, :] < lens[:, None]).astype(F32).reshape(1, 4 * 2 * slots)
    gain_hi = rounded(gain_chip)
    pack = jnp.concatenate([gain_hi, gain_chip - gain_hi])
    pack = jnp.concatenate([jnp.zeros_like(pack), pack], 1)
    pack = jnp.concatenate([pack, pack], 0)
    sent = call(
        attend_kernel,
        jax.ShapeDtypeStruct((CHIPS, 8, HEAD_SIZE), BF),
        [SMEM] + [VMEM] * 7,
        16,
        2 * 2 * 256 * 256 * 128,
        core[None],
        q,
        keys,
        values,
        keys_far,
        values_far,
        valid,
        pack,
    )
    got = exchange(sent, CHIP)
    w_side, resid, actions, new_keys, new_values, _ = lax.optimization_barrier(
        (wo_sides[0], resid, actions, step_token_keys, step_token_values, sent)
    )
    w_far = swap(w_side)
    w_mine = call(load_kernel, jax.ShapeDtypeStruct(w_side.shape, BF), [VMEM], 8, 1 << 20, w_side)
    r_chip = chip_rows(resid, swap(resid)).astype(F32)
    kv = chip // GROUP

    def fresh(x):
        x = lax.dynamic_slice(x, (0, row0, kv * HEAD_SIZE), (2, HALF, HEAD_SIZE))
        return jnp.pad(x.astype(F32), ((0, 0), (0, HALF), (0, 0)))

    part = jax.ShapeDtypeStruct((HALF, 64), BF)
    near, far = call(
        merge_kernel,
        (part, part),
        [SMEM] * 2 + [VMEM] * 4,
        16,
        CHIPS * 8 * HEAD_SIZE * 8,
        step[None],
        core[None],
        got,
        q_chip,
        fresh(new_keys),
        fresh(new_values),
    )
    share = jnp.dot(near, w_mine, preferred_element_type=F32)
    share = share + jnp.dot(far, w_far, preferred_element_type=F32)
    share = share.astype(BF).reshape(HALF, CHIPS, HEAD_SIZE).transpose(1, 0, 2)
    action = lax.dynamic_index_in_dim(actions, step, 0, keepdims=True)
    action = action - place * head.shape[1]
    share, r_chip, action = lax.optimization_barrier((share, r_chip, action))
    shares = exchange(share, CHIP)
    sent = call(
        state_kernel,
        jax.ShapeDtypeStruct((CHIPS, HALF, HEAD_SIZE), BF),
        [VMEM, VMEM],
        4,
        1 << 16,
        shares,
        r_chip,
    )
    mine = exchange(sent, CHIP)
    head_t, _ = lax.optimization_barrier((head.T, mine))
    head_t = call(load_kernel, jax.ShapeDtypeStruct(head_t.shape, BF), [VMEM], 24, 1 << 24, head_t)
    local, own = call(
        head_kernel,
        (jax.ShapeDtypeStruct((8, 128), F32), jax.ShapeDtypeStruct((8, HEAD_SIZE), BF)),
        [SMEM] * 2 + [VMEM] * 5,
        24,
        2 * 8 * D * head.shape[1],
        core[None],
        chip[None],
        mine,
        swap(mine),
        got,
        head_t,
        action,
        scratch=[pltpu.VMEM((CHIPS, 8, HEAD_SIZE), BF)],
    )
    own = jnp.where(core == 0, own[:, :64], own[:, 64:])
    peer_normed = lax.ppermute(own, "role", [(0, 1), (1, 0)])
    packed = call(
        pack_kernel,
        jax.ShapeDtypeStruct((2 * CHIPS, 1, HEAD_SIZE), F32),
        [VMEM, VMEM],
        4,
        1 << 16,
        local,
        swap(local),
    )
    heard = exchange(packed, ("role",) + CHIP)
    return call(
        final_kernel,
        (
            jax.ShapeDtypeStruct((1, 8), F32),
            jax.ShapeDtypeStruct((1, *peer_normed.shape), BF),
        ),
        [SMEM, VMEM, VMEM],
        4,
        1 << 16,
        ((1 - side) * CHIPS)[None],
        heard,
        peer_normed,
    )


def solution(mesh):
    split = Mesh(
        mesh.devices.reshape(mesh.shape["role"], mesh.shape["grp"], 4, 8, 2),
        ("role", "grp", "tp_0", "tp_1", "tp_2"),
    )
    return jax.shard_map(
        on_device,
        mesh=split,
        in_specs=(
            P(None, None, GRP_TP),
            P(),
            P(),
            P(None, GRP_TP, None),
            P(None, GRP_TP, None),
            P(),
            P("role", GRP_TP, None),
            P("role", GRP_TP),
            P(None, GRP_TP),
            P(None, None, GRP_TP),
            P(),
        ),
        out_specs=(P("role", None), P("role", None, GRP_TP)),
        check_vma=False,
    )
```

```python
import math

import jax
import jax.numpy as jnp
from jax import lax
from jax.experimental import pallas as pl
from jax.experimental.pallas import tpu as pltpu
from jax.sharding import Mesh
from jax.sharding import PartitionSpec as P

D = 8192
KV_HEADS = 8
GROUP = 8
HEAD_SIZE = 128
CHIP = ("grp", "tp_0", "tp_1")
CORE = "tp_2"
GRP_TP = CHIP + (CORE,)
CHIPS = 64
HALF = 4
LOW = -(2.0**100)
BF = jnp.bfloat16
F32 = jnp.float32


def swap(x):
    return lax.ppermute(x, CORE, [(0, 1), (1, 0)])


def exchange(x, axes):
    return lax.all_to_all(x, axes, split_axis=0, concat_axis=0, tiled=True)


def rounded(x):
    return lax.reduce_precision(x, 8, 7)


def by_core(core, mine, other, axis):
    first = jnp.concatenate([mine, other], axis)
    second = jnp.concatenate([other, mine], axis)
    return jnp.where(core == 0, first, second)


NT = (((1,), (1,)), ((), ()))
VMEM = pl.BlockSpec(memory_space=pltpu.VMEM)
SMEM = pl.BlockSpec(memory_space=pltpu.SMEM)


def call(kernel, shapes, specs, limit, cost, *operands, scratch=()):
    return pl.pallas_call(
        kernel,
        out_shape=shapes,
        in_specs=specs,
        scratch_shapes=scratch,
        out_specs=jax.tree.map(lambda _: VMEM, shapes),
        compiler_params=pltpu.CompilerParams(vmem_limit_bytes=limit * 2**20),
        cost_estimate=pl.CostEstimate(
            flops=cost, bytes_accessed=cost // 16, transcendentals=0
        ),
    )(*operands)


def load_kernel(x_ref, out_ref):
    out_ref[...] = x_ref[...]


def attend_kernel(core_ref, q_ref, k_ref, v_ref, kf_ref, vf_ref, ok_ref, pack_ref, out_ref):
    base = core_ref[0] * HALF
    row = lax.broadcasted_iota(jnp.int32, (256, 256), 0)
    col = lax.broadcasted_iota(jnp.int32, (256, 256), 1)
    valid = ((row % HALF) == (col // 64)) & (ok_ref[...] > 0)

    def both(near, far, kv):
        cols = slice(kv * HEAD_SIZE, (kv + 1) * HEAD_SIZE)
        parts = []
        for r in range(HALF):
            parts += [near[base + r, :, cols], far[base + r, :, cols]]
        return jnp.concatenate(parts, 0)

    s = jnp.concatenate(
        [
            lax.dot_general(
                q_ref[kv * 32 : (kv + 1) * 32, :],
                both(k_ref, kf_ref, kv),
                NT,
                preferred_element_type=F32,
            )
            for kv in range(KV_HEADS)
        ],
        0,
    )
    s = jnp.where(valid, s * (1.0 / math.sqrt(HEAD_SIZE)), LOW)
    top = jnp.max(s, 1, keepdims=True).astype(BF).astype(F32)
    p = jnp.where(valid, jnp.exp(s - top), 0.0)
    total = jnp.sum(p, 1, keepdims=True)
    p = p.astype(BF)
    total_hi = total.astype(BF).astype(F32)
    lane = lax.broadcasted_iota(jnp.int32, (256, 128), 1)
    stats = jnp.where(lane < 32, total_hi, total - total_hi)
    stats = jnp.where(lane < 16, top, stats)
    acc = jnp.concatenate(
        [
            jnp.dot(
                p[kv * 32 : (kv + 1) * 32],
                both(v_ref, vf_ref, kv),
                preferred_element_type=F32,
            )
            for kv in range(KV_HEADS)
        ],
        0,
    ).reshape(32, 8, 128)
    stats = jnp.where(lane.reshape(32, 8, 128) < 64, stats.reshape(32, 8, 128), pack_ref[...][None])
    upper = lax.broadcasted_iota(jnp.int32, (32, 8, 128), 1) < HALF
    even = jnp.where(upper, acc, pltpu.roll(stats, HALF, 1)).astype(BF)
    odd = jnp.where(upper, pltpu.roll(acc, HALF, 1), stats).astype(BF)
    for t in range(32):
        out_ref[2 * t] = even[t]
        out_ref[2 * t + 1] = odd[t]


def merge_kernel(step_ref, core_ref, got_ref, q_ref, fk_ref, fv_ref, near_ref, far_ref):
    x = got_ref[...].astype(F32)
    stats = pltpu.roll(x, HALF, 1)
    tops = stats[:, :, 0:1]
    totals = stats[:, :, 16:17] + stats[:, :, 32:33]
    q = q_ref[...]
    scale = 1.0 / math.sqrt(HEAD_SIZE)
    s0 = jnp.sum(fk_ref[0] * q, 1, keepdims=True) * scale
    s1 = jnp.sum(fk_ref[1] * q, 1, keepdims=True) * scale
    second = step_ref[0] >= 1
    s1 = jnp.where(second, s1, LOW)
    peak = jnp.maximum(jnp.max(tops, 0), jnp.maximum(s0, s1))
    factor = jnp.exp(tops - peak[None])
    p0 = jnp.exp(s0 - peak)
    p1 = jnp.where(second, jnp.exp(s1 - peak), 0.0)
    below = jnp.sum(totals * factor, 0) + p0 + p1
    above = jnp.sum(x * factor, 0) + p0 * fv_ref[0] + p1 * fv_ref[1]
    row = lax.broadcasted_iota(jnp.int32, (8, 128), 0)
    attended = jnp.where(row < HALF, above / below, 0.0)
    turned = pltpu.roll(attended, 64, 1)
    first = core_ref[0] == 0
    near_ref[...] = jnp.where(first, attended, turned)[:HALF, :64].astype(BF)
    far_ref[...] = jnp.where(first, turned, attended)[:HALF, :64].astype(BF)


def state_kernel(got_ref, resid_ref, out_ref):
    state = jnp.sum(got_ref[...].astype(F32), 0) + resid_ref[...]
    out_ref[...] = jnp.broadcast_to(state.astype(BF)[None], out_ref.shape)


def head_kernel(
    core_ref, chip_ref, near_ref, far_ref, got_ref, head_ref, action_ref, out_ref, own_ref, u_ref
):
    near, far = near_ref[...].astype(F32), far_ref[...].astype(F32)
    first = core_ref[0] == 0
    whole = jnp.concatenate([jnp.where(first, near, far), jnp.where(first, far, near)], 1)
    square = jnp.sum(jnp.sum(whole * whole, 0), 1, keepdims=True)
    inverse = lax.rsqrt(square / D + 1e-05)
    gain = got_ref[...].astype(F32)
    gain = gain + pltpu.roll(gain, 6, 1)
    left = lax.broadcasted_iota(jnp.int32, (CHIPS, 1, HEAD_SIZE), 2) < 64
    gain = jnp.where(left, pltpu.roll(gain[:, 4:5], 64, 2), gain[:, 5:6])
    u_ref[...] = (whole * inverse[None] * gain).astype(BF)
    own_ref[...] = u_ref[chip_ref[0]]
    u = jnp.concatenate([u_ref[i] for i in range(CHIPS)], 1)
    logits = lax.dot_general(head_ref[...], u, NT, preferred_element_type=F32)
    ids = lax.broadcasted_iota(jnp.int32, logits.shape, 0)
    high = jnp.max(logits, 0, keepdims=True)
    out_ref[...] = jnp.zeros_like(out_ref)
    out_ref[0:1, 0:8] = high
    out_ref[1:2, 0:8] = jnp.sum(jnp.exp(logits - high), 0, keepdims=True)
    out_ref[2:3, 0:8] = jnp.sum(
        jnp.where(ids == action_ref[...], logits, 0.0), 0, keepdims=True
    )


def pack_kernel(near_ref, far_ref, out_ref):
    a, b = near_ref[...], far_ref[...]
    high = jnp.maximum(a[0:1], b[0:1])
    total = a[1:2] * jnp.exp(a[0:1] - high) + b[1:2] * jnp.exp(b[0:1] - high)
    x = high + pltpu.roll(total, 8, 1) + pltpu.roll(a[2:3] + b[2:3], 16, 1)
    out_ref[...] = jnp.broadcast_to(x[None], out_ref.shape)


def final_kernel(start_ref, heard_ref, normed_ref, out_ref, normed_out):
    normed_out[...] = normed_ref[...][None]
    x = heard_ref[pl.ds(start_ref[0], CHIPS)]
    high = jnp.max(x, 0, keepdims=True)
    total = jnp.sum(pltpu.roll(x, 120, 2) * jnp.exp(x - high), 0)
    target = jnp.sum(pltpu.roll(x, 112, 2), 0)
    out_ref[...] = (target - high[0] - jnp.log(total))[:, 0:8]


def on_device(
    queries,
    step_token_keys,
    step_token_values,
    stored_key_cache,
    stored_value_cache,
    lengths,
    wo_sides,
    gain_sides,
    head,
    resid,
    actions,
):
    place = lax.axis_index(GRP_TP)
    chip = lax.axis_index(CHIP)
    core = lax.axis_index(CORE)
    side = lax.axis_index("role")
    step = 1 - side
    slots = stored_key_cache.shape[1]
    row0 = core * HALF

    def rows_of(x, start, axis=0):
        return lax.dynamic_slice_in_dim(x, start, HALF, axis)

    def chip_rows(x, far):
        near = rows_of(lax.dynamic_index_in_dim(x, step, 0, keepdims=False), row0)
        far = rows_of(lax.dynamic_index_in_dim(far, step, 0, keepdims=False), row0)
        return by_core(core, near, far, 1)

    spot = jnp.stack([step, core])
    q_half = chip_rows(queries, swap(queries))
    q_chip = jnp.pad(q_half.astype(F32), ((0, HALF), (0, 0)))
    sent = lax.optimization_barrier(
        jnp.broadcast_to(q_half[None], (CHIPS, *q_half.shape))
    )
    q = exchange(sent, CHIP).reshape(CHIPS * HALF, HEAD_SIZE)

    keys, values, lengths, gain, gain_far, _ = lax.optimization_barrier(
        (stored_key_cache, stored_value_cache, lengths, gain_sides, swap(gain_sides), sent)
    )
    keys_far, values_far = swap(keys), swap(values)
    to_self = [(0, 0), (1, 1)]
    keys, values = lax.ppermute(keys, CORE, to_self), lax.ppermute(values, CORE, to_self)
    gain_chip = by_core(core, gain, gain_far, 0)

    lens = rows_of(lengths, row0)
    at = jnp.arange(slots, dtype=jnp.int32)
    position = jnp.concatenate([place * slots + at, (place + 1 - 2 * core) * slots + at])
    valid = (position[None, :] < lens[:, None]).astype(F32).reshape(1, 4 * 2 * slots)
    gain_hi = rounded(gain_chip)
    pack = jnp.concatenate([gain_hi, gain_chip - gain_hi])
    pack = jnp.concatenate([jnp.zeros_like(pack), pack], 1)
    pack = jnp.concatenate([pack, pack], 0)
    sent = call(
        attend_kernel,
        jax.ShapeDtypeStruct((CHIPS, 8, HEAD_SIZE), BF),
        [SMEM] + [VMEM] * 7,
        16,
        2 * 2 * 256 * 256 * 128,
        core[None],
        q,
        keys,
        values,
        keys_far,
        values_far,
        valid,
        pack,
    )
    got = exchange(sent, CHIP)
    w_side, resid, actions, new_keys, new_values, _ = lax.optimization_barrier(
        (wo_sides[0], resid, actions, step_token_keys, step_token_values, sent)
    )
    w_far = swap(w_side)
    w_mine = lax.ppermute(w_side, CORE, to_self)
    r_chip = chip_rows(resid, swap(resid)).astype(F32)
    kv = chip // GROUP

    def fresh(x):
        x = lax.dynamic_slice(x, (0, row0, kv * HEAD_SIZE), (2, HALF, HEAD_SIZE))
        return jnp.pad(x.astype(F32), ((0, 0), (0, HALF), (0, 0)))

    part = jax.ShapeDtypeStruct((HALF, 64), BF)
    near, far = call(
        merge_kernel,
        (part, part),
        [SMEM] * 2 + [VMEM] * 4,
        16,
        CHIPS * 8 * HEAD_SIZE * 8,
        step[None],
        core[None],
        got,
        q_chip,
        fresh(new_keys),
        fresh(new_values),
    )
    share = jnp.dot(near, w_mine, preferred_element_type=F32)
    share = share + jnp.dot(far, w_far, preferred_element_type=F32)
    share = share.astype(BF).reshape(HALF, CHIPS, HEAD_SIZE).transpose(1, 0, 2)
    action = lax.dynamic_index_in_dim(actions, step, 0, keepdims=True)
    action = action - place * head.shape[1]
    share, r_chip, action = lax.optimization_barrier((share, r_chip, action))
    shares = exchange(share, CHIP)
    sent = call(
        state_kernel,
        jax.ShapeDtypeStruct((CHIPS, HALF, HEAD_SIZE), BF),
        [VMEM, VMEM],
        4,
        1 << 16,
        shares,
        r_chip,
    )
    mine = exchange(sent, CHIP)
    head_t, _ = lax.optimization_barrier((head.T, mine))
    head_t = call(load_kernel, jax.ShapeDtypeStruct(head_t.shape, BF), [VMEM], 24, 1 << 24, head_t)
    local, own = call(
        head_kernel,
        (jax.ShapeDtypeStruct((8, 128), F32), jax.ShapeDtypeStruct((8, HEAD_SIZE), BF)),
        [SMEM] * 2 + [VMEM] * 5,
        24,
        2 * 8 * D * head.shape[1],
        core[None],
        chip[None],
        mine,
        swap(mine),
        got,
        head_t,
        action,
        scratch=[pltpu.VMEM((CHIPS, 8, HEAD_SIZE), BF)],
    )
    own = jnp.where(core == 0, own[:, :64], own[:, 64:])
    peer_normed = lax.ppermute(own, "role", [(0, 1), (1, 0)])
    packed = call(
        pack_kernel,
        jax.ShapeDtypeStruct((2 * CHIPS, 1, HEAD_SIZE), F32),
        [VMEM, VMEM],
        4,
        1 << 16,
        local,
        swap(local),
    )
    heard = exchange(packed, ("role",) + CHIP)
    return call(
        final_kernel,
        (
            jax.ShapeDtypeStruct((1, 8), F32),
            jax.ShapeDtypeStruct((1, *peer_normed.shape), BF),
        ),
        [SMEM, VMEM, VMEM],
        4,
        1 << 16,
        ((1 - side) * CHIPS)[None],
        heard,
        peer_normed,
    )


def solution(mesh):
    split = Mesh(
        mesh.devices.reshape(mesh.shape["role"], mesh.shape["grp"], 4, 8, 2),
        ("role", "grp", "tp_0", "tp_1", "tp_2"),
    )
    return jax.shard_map(
        on_device,
        mesh=split,
        in_specs=(
            P(None, None, GRP_TP),
            P(),
            P(),
            P(None, GRP_TP, None),
            P(None, GRP_TP, None),
            P(),
            P("role", GRP_TP, None),
            P("role", GRP_TP),
            P(None, GRP_TP),
            P(None, None, GRP_TP),
            P(),
        ),
        out_specs=(P("role", None), P("role", None, GRP_TP)),
        check_vma=False,
    )
```

```python
import math

import jax
import jax.numpy as jnp
from jax import lax
from jax.experimental import pallas as pl
from jax.experimental.pallas import tpu as pltpu
from jax.sharding import Mesh
from jax.sharding import PartitionSpec as P

D = 8192
KV_HEADS = 8
GROUP = 8
HEAD_SIZE = 128
CHIP = ("grp", "tp_0", "tp_1")
CORE = "tp_2"
GRP_TP = CHIP + (CORE,)
CHIPS = 64
HALF = 4
LOW = -(2.0**100)
BF = jnp.bfloat16
F32 = jnp.float32


def swap(x):
    return lax.ppermute(x, CORE, [(0, 1), (1, 0)])


def exchange(x, axes):
    return lax.all_to_all(x, axes, split_axis=0, concat_axis=0, tiled=True)


def rounded(x):
    return lax.reduce_precision(x, 8, 7)


def by_core(core, mine, other, axis):
    first = jnp.concatenate([mine, other], axis)
    second = jnp.concatenate([other, mine], axis)
    return jnp.where(core == 0, first, second)


NT = (((1,), (1,)), ((), ()))
VMEM = pl.BlockSpec(memory_space=pltpu.VMEM)
SMEM = pl.BlockSpec(memory_space=pltpu.SMEM)


def call(kernel, shapes, specs, limit, cost, *operands, scratch=()):
    return pl.pallas_call(
        kernel,
        out_shape=shapes,
        in_specs=specs,
        scratch_shapes=scratch,
        out_specs=jax.tree.map(lambda _: VMEM, shapes),
        compiler_params=pltpu.CompilerParams(vmem_limit_bytes=limit * 2**20),
        cost_estimate=pl.CostEstimate(
            flops=cost, bytes_accessed=cost // 16, transcendentals=0
        ),
    )(*operands)


def load_kernel(x_ref, out_ref):
    out_ref[...] = x_ref[...]


def attend_kernel(core_ref, q_ref, k_ref, v_ref, kf_ref, vf_ref, ok_ref, pack_ref, out_ref):
    base = core_ref[0] * HALF
    row = lax.broadcasted_iota(jnp.int32, (256, 256), 0)
    col = lax.broadcasted_iota(jnp.int32, (256, 256), 1)
    valid = ((row % HALF) == (col // 64)) & (ok_ref[...] > 0)

    def both(near, far, kv):
        cols = slice(kv * HEAD_SIZE, (kv + 1) * HEAD_SIZE)
        parts = []
        for r in range(HALF):
            parts += [near[r, :, cols], far[base + r, :, cols]]
        return jnp.concatenate(parts, 0)

    s = jnp.concatenate(
        [
            lax.dot_general(
                q_ref[kv * 32 : (kv + 1) * 32, :],
                both(k_ref, kf_ref, kv),
                NT,
                preferred_element_type=F32,
            )
            for kv in range(KV_HEADS)
        ],
        0,
    )
    s = jnp.where(valid, s * (1.0 / math.sqrt(HEAD_SIZE)), LOW)
    top = jnp.max(s, 1, keepdims=True).astype(BF).astype(F32)
    p = jnp.where(valid, jnp.exp(s - top), 0.0)
    total = jnp.sum(p, 1, keepdims=True)
    p = p.astype(BF)
    total_hi = total.astype(BF).astype(F32)
    lane = lax.broadcasted_iota(jnp.int32, (256, 128), 1)
    stats = jnp.where(lane < 32, total_hi, total - total_hi)
    stats = jnp.where(lane < 16, top, stats)
    acc = jnp.concatenate(
        [
            jnp.dot(
                p[kv * 32 : (kv + 1) * 32],
                both(v_ref, vf_ref, kv),
                preferred_element_type=F32,
            )
            for kv in range(KV_HEADS)
        ],
        0,
    ).reshape(32, 8, 128)
    stats = jnp.where(lane.reshape(32, 8, 128) < 64, stats.reshape(32, 8, 128), pack_ref[...][None])
    upper = lax.broadcasted_iota(jnp.int32, (32, 8, 128), 1) < HALF
    even = jnp.where(upper, acc, pltpu.roll(stats, HALF, 1)).astype(BF)
    odd = jnp.where(upper, pltpu.roll(acc, HALF, 1), stats).astype(BF)
    for t in range(32):
        out_ref[2 * t] = even[t]
        out_ref[2 * t + 1] = odd[t]


def merge_kernel(step_ref, core_ref, got_ref, q_ref, fk_ref, fv_ref, near_ref, far_ref):
    x = got_ref[...].astype(F32)
    stats = pltpu.roll(x, HALF, 1)
    tops = stats[:, :, 0:1]
    totals = stats[:, :, 16:17] + stats[:, :, 32:33]
    q = q_ref[...]
    scale = 1.0 / math.sqrt(HEAD_SIZE)
    s0 = jnp.sum(fk_ref[0] * q, 1, keepdims=True) * scale
    s1 = jnp.sum(fk_ref[1] * q, 1, keepdims=True) * scale
    second = step_ref[0] >= 1
    s1 = jnp.where(second, s1, LOW)
    peak = jnp.maximum(jnp.max(tops, 0), jnp.maximum(s0, s1))
    factor = jnp.exp(tops - peak[None])
    p0 = jnp.exp(s0 - peak)
    p1 = jnp.where(second, jnp.exp(s1 - peak), 0.0)
    below = jnp.sum(totals * factor, 0) + p0 + p1
    above = jnp.sum(x * factor, 0) + p0 * fv_ref[0] + p1 * fv_ref[1]
    row = lax.broadcasted_iota(jnp.int32, (8, 128), 0)
    attended = jnp.where(row < HALF, above / below, 0.0)
    turned = pltpu.roll(attended, 64, 1)
    first = core_ref[0] == 0
    near_ref[...] = jnp.where(first, attended, turned)[:HALF, :64].astype(BF)
    far_ref[...] = jnp.where(first, turned, attended)[:HALF, :64].astype(BF)


def state_kernel(got_ref, resid_ref, out_ref):
    state = jnp.sum(got_ref[...].astype(F32), 0) + resid_ref[...]
    out_ref[...] = jnp.broadcast_to(state.astype(BF)[None], out_ref.shape)


def head_kernel(
    core_ref, chip_ref, step_ref, base_ref, near_ref, far_ref, got_ref, head_ref, action_ref, out_ref, own_ref, u_ref
):
    near, far = near_ref[...].astype(F32), far_ref[...].astype(F32)
    first = core_ref[0] == 0
    whole = jnp.concatenate([jnp.where(first, near, far), jnp.where(first, far, near)], 1)
    square = jnp.sum(jnp.sum(whole * whole, 0), 1, keepdims=True)
    inverse = lax.rsqrt(square / D + 1e-05)
    gain = got_ref[...].astype(F32)
    gain = gain + pltpu.roll(gain, 6, 1)
    left = lax.broadcasted_iota(jnp.int32, (CHIPS, 1, HEAD_SIZE), 2) < 64
    gain = jnp.where(left, pltpu.roll(gain[:, 4:5], 64, 2), gain[:, 5:6])
    u_ref[...] = (whole * inverse[None] * gain).astype(BF)
    own_ref[...] = u_ref[chip_ref[0]]
    u = jnp.concatenate([u_ref[i] for i in range(CHIPS)], 1)
    logits = lax.dot_general(head_ref[...], u, NT, preferred_element_type=F32)
    ids = lax.broadcasted_iota(jnp.int32, logits.shape, 0)
    action = jnp.where(step_ref[0] == 0, action_ref[0:1, :], action_ref[1:2, :])
    high = jnp.max(logits, 0, keepdims=True)
    out_ref[...] = jnp.zeros_like(out_ref)
    out_ref[0:1, 0:8] = high
    out_ref[1:2, 0:8] = jnp.sum(jnp.exp(logits - high), 0, keepdims=True)
    out_ref[2:3, 0:8] = jnp.sum(
        jnp.where(ids + base_ref[0] == action, logits, 0.0), 0, keepdims=True
    )


def pack_kernel(near_ref, far_ref, out_ref):
    a, b = near_ref[...], far_ref[...]
    high = jnp.maximum(a[0:1], b[0:1])
    total = a[1:2] * jnp.exp(a[0:1] - high) + b[1:2] * jnp.exp(b[0:1] - high)
    x = high + pltpu.roll(total, 8, 1) + pltpu.roll(a[2:3] + b[2:3], 16, 1)
    out_ref[...] = jnp.broadcast_to(x[None], out_ref.shape)


def final_kernel(start_ref, heard_ref, normed_ref, out_ref, normed_out):
    normed_out[...] = normed_ref[...][None]
    x = heard_ref[pl.ds(start_ref[0], CHIPS)]
    high = jnp.max(x, 0, keepdims=True)
    total = jnp.sum(pltpu.roll(x, 120, 2) * jnp.exp(x - high), 0)
    target = jnp.sum(pltpu.roll(x, 112, 2), 0)
    out_ref[...] = (target - high[0] - jnp.log(total))[:, 0:8]


def on_device(
    queries,
    step_token_keys,
    step_token_values,
    stored_key_cache,
    stored_value_cache,
    lengths,
    wo_sides,
    gain_sides,
    head,
    resid,
    actions,
):
    place = lax.axis_index(GRP_TP)
    chip = lax.axis_index(CHIP)
    core = lax.axis_index(CORE)
    side = lax.axis_index("role")
    step = 1 - side
    slots = stored_key_cache.shape[1]
    row0 = core * HALF

    def rows_of(x, start, axis=0):
        return lax.dynamic_slice_in_dim(x, start, HALF, axis)

    def chip_rows(x, far):
        near = rows_of(lax.dynamic_index_in_dim(x, step, 0, keepdims=False), row0)
        far = rows_of(lax.dynamic_index_in_dim(far, step, 0, keepdims=False), row0)
        return by_core(core, near, far, 1)

    spot = jnp.stack([step, core])
    q_half = chip_rows(queries, swap(queries))
    q_chip = jnp.pad(q_half.astype(F32), ((0, HALF), (0, 0)))
    sent = lax.optimization_barrier(
        jnp.broadcast_to(q_half[None], (CHIPS, *q_half.shape))
    )
    q = exchange(sent, CHIP).reshape(CHIPS * HALF, HEAD_SIZE)

    keys, values, lengths, gain, gain_far, _ = lax.optimization_barrier(
        (stored_key_cache, stored_value_cache, lengths, gain_sides, swap(gain_sides), sent)
    )
    keys_far, values_far = swap(keys), swap(values)
    keys, values = rows_of(keys, row0), rows_of(values, row0)
    gain_chip = by_core(core, gain, gain_far, 0)

    lens = rows_of(lengths, row0)
    at = jnp.arange(slots, dtype=jnp.int32)
    position = jnp.concatenate([place * slots + at, (place + 1 - 2 * core) * slots + at])
    valid = (position[None, :] < lens[:, None]).astype(F32).reshape(1, 4 * 2 * slots)
    gain_hi = rounded(gain_chip)
    pack = jnp.concatenate([gain_hi, gain_chip - gain_hi])
    pack = jnp.concatenate([jnp.zeros_like(pack), pack], 1)
    pack = jnp.concatenate([pack, pack], 0)
    sent = call(
        attend_kernel,
        jax.ShapeDtypeStruct((CHIPS, 8, HEAD_SIZE), BF),
        [SMEM] + [VMEM] * 7,
        16,
        2 * 2 * 256 * 256 * 128,
        core[None],
        q,
        keys,
        values,
        keys_far,
        values_far,
        valid,
        pack,
    )
    got = exchange(sent, CHIP)
    w_side, resid, actions, new_keys, new_values, _ = lax.optimization_barrier(
        (wo_sides[0], resid, actions, step_token_keys, step_token_values, sent)
    )
    w_far = swap(w_side)
    w_mine = call(load_kernel, jax.ShapeDtypeStruct(w_side.shape, BF), [VMEM], 8, 1 << 20, w_side)
    r_chip = chip_rows(resid, swap(resid)).astype(F32)
    kv = chip // GROUP

    def fresh(x):
        x = lax.dynamic_slice(x, (0, row0, kv * HEAD_SIZE), (2, HALF, HEAD_SIZE))
        return jnp.pad(x.astype(F32), ((0, 0), (0, HALF), (0, 0)))

    part = jax.ShapeDtypeStruct((HALF, 64), BF)
    near, far = call(
        merge_kernel,
        (part, part),
        [SMEM] * 2 + [VMEM] * 4,
        16,
        CHIPS * 8 * HEAD_SIZE * 8,
        step[None],
        core[None],
        got,
        q_chip,
        fresh(new_keys),
        fresh(new_values),
    )
    share = jnp.dot(near, w_mine, preferred_element_type=F32)
    share = share + jnp.dot(far, w_far, preferred_element_type=F32)
    share = share.astype(BF).reshape(HALF, CHIPS, HEAD_SIZE).transpose(1, 0, 2)
    share, r_chip = lax.optimization_barrier((share, r_chip))
    shares = exchange(share, CHIP)
    sent = call(
        state_kernel,
        jax.ShapeDtypeStruct((CHIPS, HALF, HEAD_SIZE), BF),
        [VMEM, VMEM],
        4,
        1 << 16,
        shares,
        r_chip,
    )
    mine = exchange(sent, CHIP)
    head_t, _ = lax.optimization_barrier((head.T, mine))
    head_t = call(load_kernel, jax.ShapeDtypeStruct(head_t.shape, BF), [VMEM], 24, 1 << 24, head_t)
    local, own = call(
        head_kernel,
        (jax.ShapeDtypeStruct((8, 128), F32), jax.ShapeDtypeStruct((8, HEAD_SIZE), BF)),
        [SMEM] * 4 + [VMEM] * 5,
        24,
        2 * 8 * D * head.shape[1],
        core[None],
        chip[None],
        step[None],
        (place * head.shape[1])[None],
        mine,
        swap(mine),
        got,
        head_t,
        actions,
        scratch=[pltpu.VMEM((CHIPS, 8, HEAD_SIZE), BF)],
    )
    own = jnp.where(core == 0, own[:, :64], own[:, 64:])
    peer_normed = lax.ppermute(own, "role", [(0, 1), (1, 0)])
    packed = call(
        pack_kernel,
        jax.ShapeDtypeStruct((2 * CHIPS, 1, HEAD_SIZE), F32),
        [VMEM, VMEM],
        4,
        1 << 16,
        local,
        swap(local),
    )
    heard = exchange(packed, ("role",) + CHIP)
    return call(
        final_kernel,
        (
            jax.ShapeDtypeStruct((1, 8), F32),
            jax.ShapeDtypeStruct((1, *peer_normed.shape), BF),
        ),
        [SMEM, VMEM, VMEM],
        4,
        1 << 16,
        ((1 - side) * CHIPS)[None],
        heard,
        peer_normed,
    )


def solution(mesh):
    split = Mesh(
        mesh.devices.reshape(mesh.shape["role"], mesh.shape["grp"], 4, 8, 2),
        ("role", "grp", "tp_0", "tp_1", "tp_2"),
    )
    return jax.shard_map(
        on_device,
        mesh=split,
        in_specs=(
            P(None, None, GRP_TP),
            P(),
            P(),
            P(None, GRP_TP, None),
            P(None, GRP_TP, None),
            P(),
            P("role", GRP_TP, None),
            P("role", GRP_TP),
            P(None, GRP_TP),
            P(None, None, GRP_TP),
            P(),
        ),
        out_specs=(P("role", None), P("role", None, GRP_TP)),
        check_vma=False,
    )
```

```python
import math

import jax
import jax.numpy as jnp
from jax import lax
from jax.experimental import pallas as pl
from jax.experimental.pallas import tpu as pltpu
from jax.sharding import Mesh
from jax.sharding import PartitionSpec as P

D = 8192
KV_HEADS = 8
GROUP = 8
HEAD_SIZE = 128
CHIP = ("grp", "tp_0", "tp_1")
CORE = "tp_2"
GRP_TP = CHIP + (CORE,)
CHIPS = 64
HALF = 4
LOW = -(2.0**100)
BF = jnp.bfloat16
F32 = jnp.float32


def swap(x):
    return lax.ppermute(x, CORE, [(0, 1), (1, 0)])


def exchange(x, axes):
    return lax.all_to_all(x, axes, split_axis=0, concat_axis=0, tiled=True)


def rounded(x):
    return lax.reduce_precision(x, 8, 7)


def by_core(core, mine, other, axis):
    first = jnp.concatenate([mine, other], axis)
    second = jnp.concatenate([other, mine], axis)
    return jnp.where(core == 0, first, second)


NT = (((1,), (1,)), ((), ()))
VMEM = pl.BlockSpec(memory_space=pltpu.VMEM)
SMEM = pl.BlockSpec(memory_space=pltpu.SMEM)


def call(kernel, shapes, specs, limit, cost, *operands, scratch=()):
    return pl.pallas_call(
        kernel,
        out_shape=shapes,
        in_specs=specs,
        scratch_shapes=scratch,
        out_specs=jax.tree.map(lambda _: VMEM, shapes),
        compiler_params=pltpu.CompilerParams(vmem_limit_bytes=limit * 2**20),
        cost_estimate=pl.CostEstimate(
            flops=cost, bytes_accessed=cost // 16, transcendentals=0
        ),
    )(*operands)


def load_kernel(x_ref, out_ref):
    out_ref[...] = x_ref[...]


def attend_kernel(core_ref, q_ref, k_ref, v_ref, kf_ref, vf_ref, ok_ref, pack_ref, out_ref):
    base = core_ref[0] * HALF
    row = lax.broadcasted_iota(jnp.int32, (256, 256), 0)
    col = lax.broadcasted_iota(jnp.int32, (256, 256), 1)
    valid = ((row % HALF) == (col // 64)) & (ok_ref[...] > 0)

    def both(near, far, kv):
        cols = slice(kv * HEAD_SIZE, (kv + 1) * HEAD_SIZE)
        parts = []
        for r in range(HALF):
            parts += [near[r, :, cols], far[base + r, :, cols]]
        return jnp.concatenate(parts, 0)

    s = jnp.concatenate(
        [
            lax.dot_general(
                q_ref[kv * 32 : (kv + 1) * 32, :],
                both(k_ref, kf_ref, kv),
                NT,
                preferred_element_type=F32,
            )
            for kv in range(KV_HEADS)
        ],
        0,
    )
    s = jnp.where(valid, s * (1.0 / math.sqrt(HEAD_SIZE)), LOW)
    top = jnp.max(s, 1, keepdims=True).astype(BF).astype(F32)
    p = jnp.where(valid, jnp.exp(s - top), 0.0)
    total = jnp.sum(p, 1, keepdims=True)
    p = p.astype(BF)
    total_hi = total.astype(BF).astype(F32)
    lane = lax.broadcasted_iota(jnp.int32, (256, 128), 1)
    stats = jnp.where(lane < 32, total_hi, total - total_hi)
    stats = jnp.where(lane < 16, top, stats)
    acc = jnp.concatenate(
        [
            jnp.dot(
                p[kv * 32 : (kv + 1) * 32],
                both(v_ref, vf_ref, kv),
                preferred_element_type=F32,
            )
            for kv in range(KV_HEADS)
        ],
        0,
    ).reshape(32, 8, 128)
    stats = jnp.where(lane.reshape(32, 8, 128) < 64, stats.reshape(32, 8, 128), pack_ref[...][None])
    upper = lax.broadcasted_iota(jnp.int32, (32, 8, 128), 1) < HALF
    even = jnp.where(upper, acc, pltpu.roll(stats, HALF, 1)).astype(BF)
    odd = jnp.where(upper, pltpu.roll(acc, HALF, 1), stats).astype(BF)
    for t in range(32):
        out_ref[2 * t] = even[t]
        out_ref[2 * t + 1] = odd[t]


def merge_kernel(step_ref, core_ref, got_ref, q_ref, fk_ref, fv_ref, near_ref, far_ref):
    x = got_ref[...].astype(F32)
    stats = pltpu.roll(x, HALF, 1)
    tops = stats[:, :, 0:1]
    totals = stats[:, :, 16:17] + stats[:, :, 32:33]
    q = q_ref[...]
    scale = 1.0 / math.sqrt(HEAD_SIZE)
    s0 = jnp.sum(fk_ref[0] * q, 1, keepdims=True) * scale
    s1 = jnp.sum(fk_ref[1] * q, 1, keepdims=True) * scale
    second = step_ref[0] >= 1
    s1 = jnp.where(second, s1, LOW)
    peak = jnp.maximum(jnp.max(tops, 0), jnp.maximum(s0, s1))
    factor = jnp.exp(tops - peak[None])
    p0 = jnp.exp(s0 - peak)
    p1 = jnp.where(second, jnp.exp(s1 - peak), 0.0)
    below = jnp.sum(totals * factor, 0) + p0 + p1
    above = jnp.sum(x * factor, 0) + p0 * fv_ref[0] + p1 * fv_ref[1]
    row = lax.broadcasted_iota(jnp.int32, (8, 128), 0)
    attended = jnp.where(row < HALF, above / below, 0.0)
    turned = pltpu.roll(attended, 64, 1)
    first = core_ref[0] == 0
    near_ref[...] = jnp.where(first, attended, turned)[:HALF, :64].astype(BF)
    far_ref[...] = jnp.where(first, turned, attended)[:HALF, :64].astype(BF)


def state_kernel(got_ref, resid_ref, out_ref):
    state = jnp.sum(got_ref[...].astype(F32), 0) + resid_ref[...]
    out_ref[...] = jnp.broadcast_to(state.astype(BF)[None], out_ref.shape)


def head_kernel(
    core_ref, chip_ref, near_ref, far_ref, got_ref, head_ref, action_ref, out_ref, own_ref, u_ref
):
    near, far = near_ref[...].astype(F32), far_ref[...].astype(F32)
    first = core_ref[0] == 0
    whole = jnp.concatenate([jnp.where(first, near, far), jnp.where(first, far, near)], 1)
    square = jnp.sum(jnp.sum(whole * whole, 0), 1, keepdims=True)
    inverse = lax.rsqrt(square / D + 1e-05)
    gain = got_ref[...].astype(F32)
    gain = gain + pltpu.roll(gain, 6, 1)
    left = lax.broadcasted_iota(jnp.int32, (CHIPS, 1, HEAD_SIZE), 2) < 64
    gain = jnp.where(left, pltpu.roll(gain[:, 4:5], 64, 2), gain[:, 5:6])
    u_ref[...] = (whole * inverse[None] * gain).astype(BF)
    own_ref[...] = u_ref[chip_ref[0]]
    u = jnp.concatenate([u_ref[i] for i in range(CHIPS)], 1)
    logits = lax.dot_general(head_ref[...], u, NT, preferred_element_type=F32)
    ids = lax.broadcasted_iota(jnp.int32, logits.shape, 0)
    high = jnp.max(logits, 0, keepdims=True)
    out_ref[...] = jnp.zeros_like(out_ref)
    out_ref[0:1, 0:8] = high
    out_ref[1:2, 0:8] = jnp.sum(jnp.exp(logits - high), 0, keepdims=True)
    out_ref[2:3, 0:8] = jnp.sum(
        jnp.where(ids == action_ref[...], logits, 0.0), 0, keepdims=True
    )


def pack_kernel(near_ref, far_ref, out_ref):
    a, b = near_ref[...], far_ref[...]
    high = jnp.maximum(a[0:1], b[0:1])
    total = a[1:2] * jnp.exp(a[0:1] - high) + b[1:2] * jnp.exp(b[0:1] - high)
    x = high + pltpu.roll(total, 8, 1) + pltpu.roll(a[2:3] + b[2:3], 16, 1)
    out_ref[...] = jnp.broadcast_to(x[None], out_ref.shape)


def final_kernel(start_ref, heard_ref, normed_ref, out_ref, normed_out):
    normed_out[...] = normed_ref[...][None]
    x = heard_ref[pl.ds(start_ref[0], CHIPS)]
    high = jnp.max(x, 0, keepdims=True)
    total = jnp.sum(pltpu.roll(x, 120, 2) * jnp.exp(x - high), 0)
    target = jnp.sum(pltpu.roll(x, 112, 2), 0)
    out_ref[...] = (target - high[0] - jnp.log(total))[:, 0:8]


def on_device(
    queries,
    step_token_keys,
    step_token_values,
    stored_key_cache,
    stored_value_cache,
    lengths,
    wo_sides,
    gain_sides,
    head,
    resid,
    actions,
):
    place = lax.axis_index(GRP_TP)
    chip = lax.axis_index(CHIP)
    core = lax.axis_index(CORE)
    side = lax.axis_index("role")
    step = 1 - side
    slots = stored_key_cache.shape[1]
    row0 = core * HALF

    def rows_of(x, start, axis=0):
        return lax.dynamic_slice_in_dim(x, start, HALF, axis)

    def chip_rows(x, far):
        near = rows_of(lax.dynamic_index_in_dim(x, step, 0, keepdims=False), row0)
        far = rows_of(lax.dynamic_index_in_dim(far, step, 0, keepdims=False), row0)
        return by_core(core, near, far, 1)

    spot = jnp.stack([step, core])
    q_half = chip_rows(queries, swap(queries))
    q_chip = jnp.pad(q_half.astype(F32), ((0, HALF), (0, 0)))
    sent = lax.optimization_barrier(
        jnp.broadcast_to(q_half[None], (CHIPS, *q_half.shape))
    )
    q = exchange(sent, CHIP).reshape(CHIPS * HALF, HEAD_SIZE)

    keys, values, lengths, gain, gain_far, _ = lax.optimization_barrier(
        (stored_key_cache, stored_value_cache, lengths, gain_sides, swap(gain_sides), sent)
    )
    keys_far, values_far = swap(keys), swap(values)
    keys, values = rows_of(keys, row0), rows_of(values, row0)
    gain_chip = by_core(core, gain, gain_far, 0)

    lens = jnp.where(core == 0, lengths[:HALF], lengths[HALF:])
    at = jnp.arange(slots, dtype=jnp.int32)
    position = jnp.concatenate([place * slots + at, (place + 1 - 2 * core) * slots + at])
    valid = (position[None, :] < lens[:, None]).astype(F32).reshape(1, 4 * 2 * slots)
    gain_hi = rounded(gain_chip)
    pack = jnp.concatenate([gain_hi, gain_chip - gain_hi])
    pack = jnp.concatenate([jnp.zeros_like(pack), pack], 1)
    pack = jnp.concatenate([pack, pack], 0)
    sent = call(
        attend_kernel,
        jax.ShapeDtypeStruct((CHIPS, 8, HEAD_SIZE), BF),
        [SMEM] + [VMEM] * 7,
        16,
        2 * 2 * 256 * 256 * 128,
        core[None],
        q,
        keys,
        values,
        keys_far,
        values_far,
        valid,
        pack,
    )
    got = exchange(sent, CHIP)
    w_side, resid, actions, new_keys, new_values, _ = lax.optimization_barrier(
        (wo_sides[0], resid, actions, step_token_keys, step_token_values, sent)
    )
    w_far = swap(w_side)
    w_mine = call(load_kernel, jax.ShapeDtypeStruct(w_side.shape, BF), [VMEM], 8, 1 << 20, w_side)
    r_chip = chip_rows(resid, swap(resid)).astype(F32)
    kv = chip // GROUP

    def fresh(x):
        x = lax.dynamic_slice(x, (0, row0, kv * HEAD_SIZE), (2, HALF, HEAD_SIZE))
        return jnp.pad(x.astype(F32), ((0, 0), (0, HALF), (0, 0)))

    part = jax.ShapeDtypeStruct((HALF, 64), BF)
    near, far = call(
        merge_kernel,
        (part, part),
        [SMEM] * 2 + [VMEM] * 4,
        16,
        CHIPS * 8 * HEAD_SIZE * 8,
        step[None],
        core[None],
        got,
        q_chip,
        fresh(new_keys),
        fresh(new_values),
    )
    share = jnp.dot(near, w_mine, preferred_element_type=F32)
    share = share + jnp.dot(far, w_far, preferred_element_type=F32)
    share = share.astype(BF).reshape(HALF, CHIPS, HEAD_SIZE).transpose(1, 0, 2)
    action = lax.dynamic_index_in_dim(actions, step, 0, keepdims=True)
    action = action - place * head.shape[1]
    share, r_chip, action = lax.optimization_barrier((share, r_chip, action))
    shares = exchange(share, CHIP)
    sent = call(
        state_kernel,
        jax.ShapeDtypeStruct((CHIPS, HALF, HEAD_SIZE), BF),
        [VMEM, VMEM],
        4,
        1 << 16,
        shares,
        r_chip,
    )
    mine = exchange(sent, CHIP)
    head_t, _ = lax.optimization_barrier((head.T, mine))
    head_t = call(load_kernel, jax.ShapeDtypeStruct(head_t.shape, BF), [VMEM], 24, 1 << 24, head_t)
    local, own = call(
        head_kernel,
        (jax.ShapeDtypeStruct((8, 128), F32), jax.ShapeDtypeStruct((8, HEAD_SIZE), BF)),
        [SMEM] * 2 + [VMEM] * 5,
        24,
        2 * 8 * D * head.shape[1],
        core[None],
        chip[None],
        mine,
        swap(mine),
        got,
        head_t,
        action,
        scratch=[pltpu.VMEM((CHIPS, 8, HEAD_SIZE), BF)],
    )
    own = jnp.where(core == 0, own[:, :64], own[:, 64:])
    peer_normed = lax.ppermute(own, "role", [(0, 1), (1, 0)])
    packed = call(
        pack_kernel,
        jax.ShapeDtypeStruct((2 * CHIPS, 1, HEAD_SIZE), F32),
        [VMEM, VMEM],
        4,
        1 << 16,
        local,
        swap(local),
    )
    heard = exchange(packed, ("role",) + CHIP)
    return call(
        final_kernel,
        (
            jax.ShapeDtypeStruct((1, 8), F32),
            jax.ShapeDtypeStruct((1, *peer_normed.shape), BF),
        ),
        [SMEM, VMEM, VMEM],
        4,
        1 << 16,
        ((1 - side) * CHIPS)[None],
        heard,
        peer_normed,
    )


def solution(mesh):
    split = Mesh(
        mesh.devices.reshape(mesh.shape["role"], mesh.shape["grp"], 4, 8, 2),
        ("role", "grp", "tp_0", "tp_1", "tp_2"),
    )
    return jax.shard_map(
        on_device,
        mesh=split,
        in_specs=(
            P(None, None, GRP_TP),
            P(),
            P(),
            P(None, GRP_TP, None),
            P(None, GRP_TP, None),
            P(),
            P("role", GRP_TP, None),
            P("role", GRP_TP),
            P(None, GRP_TP),
            P(None, None, GRP_TP),
            P(),
        ),
        out_specs=(P("role", None), P("role", None, GRP_TP)),
        check_vma=False,
    )
```
